128 devices in a mesh: gx: 16 (over x, z), gy: 8 (over y, core).
Axes of the slice: x: 4, y: 4, z: 4, core: 2. Of those that a mesh axis runs over, the one named last changes fastest.
Arguments:
- rhs_state: float32 [256, 512, 256], P('gx', 'gy'), may hold values from -100 to 100
- rhs_control: float32 [256, 512, 256], P('gx', 'gy'), may hold values from -100 to 100
- rhs_adjoint: float32 [256, 512, 256], P('gx', 'gy'), may hold values from -100 to 100
- barrier: float32 [256, 512, 256], P('gx', 'gy'), may hold values from 0.1 to 10
- active: int32 [256, 512, 256], P('gx', 'gy'), may hold values 0 or 1
Outputs:
- step_state: float32 [256, 512, 256], P('gx', 'gy')
- step_control: float32 [256, 512, 256], P('gx', 'gy')
- step_adjoint: float32 [256, 512, 256], P('gx', 'gy')
The draws below stay inside these ranges and needn't reach their ends.
All inputs are finite; a program needn't handle non-finite values. No bound on the sum of `active` on one device may be relied on, other than what follows from the above.
Results may differ from the reference program's by a relative error of at most 0.0002.
Values sent between devices are 32-bit elements; how exact they have to be, the bound alone decides.
A program may use at most 64 MiB of HBM per device.

```python
import math
import jax
import jax.numpy as jnp

CZ = 256
ITERS = 2
CHEB = 2
NX = 256
NY = 512


def textured(key, base, amount):
    key_rows, key_cols = jax.random.split(key)
    row_scale = jnp.exp(jax.random.uniform(key_rows, (NX, 1, 1)) * (0.5 * math.log(10.0)))
    col_scale = jnp.exp(jax.random.uniform(key_cols, (1, NY, 1)) * (0.5 * math.log(10.0)))
    xpos = jnp.arange(NX, dtype=jnp.float32).reshape(NX, 1, 1) / NX
    ypos = jnp.arange(NY, dtype=jnp.float32).reshape(1, NY, 1) / NY
    ramp = jnp.exp(math.log(3.0) * 0.5 * (xpos + ypos))
    return (amount * base * row_scale * col_scale * ramp).astype(jnp.float32)


def drawn_field(key):
    key_base, key_rest = jax.random.split(key)
    base = jnp.clip(jax.random.normal(key_base, (NX, NY, CZ)), -6.0, 6.0)
    return textured(key_rest, base, 0.3)


def draw_rhs_state(key, part):
    key = jax.random.fold_in(key, 11)
    return drawn_field(key)


def draw_rhs_control(key, part):
    key = jax.random.fold_in(key, 23)
    return drawn_field(key)


def draw_rhs_adjoint(key, part):
    key = jax.random.fold_in(key, 37)
    return drawn_field(key)


def set_ends(drawn, stream_key, least, high):
    place = [jax.random.randint(jax.random.fold_in(stream_key, axis), (), 0, length) for axis, length in enumerate(drawn.shape)]
    main_axis = drawn.shape.index(max(drawn.shape))
    next_to = place[:main_axis] + [(place[main_axis] + 1) % drawn.shape[main_axis]] + place[main_axis + 1:]
    return drawn.at[tuple(place)].set(least).at[tuple(next_to)].set(high)


def block_levels(stream_key, extent, cuts, least, top_value):
    def one(dim, blocks):
        draws = jax.random.uniform(jax.random.fold_in(jax.random.fold_in(stream_key, 6), dim), (blocks,), jnp.float32, least / len(cuts), top_value / len(cuts))
        return jnp.repeat(jnp.exp(draws), extent[dim] // blocks).reshape((-1,) + (1,) * (len(extent) - dim - 1))

    factor_of = one(*cuts[0])
    for cut in cuts[1:]:
        factor_of = factor_of * one(*cut)
    return factor_of


def setup_inputs(seed: int = 0) -> dict:
    key_of = jax.random.split(jax.random.key(seed), 6)
    return {
        "rhs_state": draw_rhs_state(jax.random.fold_in(key_of[5], 71), 0),
        "rhs_control": draw_rhs_control(jax.random.fold_in(key_of[5], 71), 0),
        "rhs_adjoint": draw_rhs_adjoint(jax.random.fold_in(key_of[5], 71), 0),
        "barrier": jnp.clip(jnp.exp(math.log(10.0) - 4.6051702 * jax.random.uniform(key_of[3], (NX, NY, CZ), jnp.float32) ** block_levels(key_of[3], (NX, NY, CZ), ((0, 16), (1, 8)), -0.2, 0.2)), 0.1, 10.0),
        "active": set_ends((jax.random.randint(key_of[4], (NX, NY, CZ), 0, 4) < 1).astype(jnp.int32), jax.random.fold_in(key_of[4], 1), 0, 1),
    }


regular = 0.01
lower_edge = 0.5
upper_edge = 15.5

def laplace(values, damping):
    neighbours = jnp.roll(values, 1, 0) + jnp.roll(values, -1, 0)
    padded = jnp.pad(values, ((0, 0), (1, 1), (1, 1)))
    neighbours = neighbours + padded[:, 2:, 1:-1] + padded[:, :-2, 1:-1] + padded[:, 1:-1, 2:] + padded[:, 1:-1, :-2]
    return (6.0 + damping) * values - neighbours

def chebyshev(rhs, damping):
    centre = 0.5 * (upper_edge + lower_edge)
    half_span = 0.5 * (upper_edge - lower_edge)
    stretch = centre / half_span
    approx = rhs / centre
    heading = approx
    ratio_old = 1.0 / stretch
    for counter in range(CHEB):
        residual = rhs - laplace(approx, damping)
        ratio_now = 1.0 / (2.0 * stretch - ratio_old)
        heading = ratio_now * ratio_old * heading + 2.0 * ratio_now / half_span * residual
        approx = approx + heading
        ratio_old = ratio_now
    return approx

def local_inner(first, second):
    return jnp.sum(first[0] * second[0]) + jnp.sum(first[1] * second[1]) + jnp.sum(first[2] * second[2])

def reference(rhs_state, rhs_control, rhs_adjoint, barrier, active):
    fixed_mask = active.astype(jnp.float32)
    open_mask = 1.0 - fixed_mask
    control_diag = open_mask * (regular + barrier) + fixed_mask
    damping = open_mask / jnp.sqrt(regular + barrier)

    def apply_kkt(vector):
        state_part, control, adjoint = vector
        return (state_part + laplace(adjoint, 0.0), open_mask * ((regular + barrier) * control - adjoint) + fixed_mask * control, laplace(state_part, 0.0) - open_mask * control)

    def precondition(vector):
        return (vector[0], vector[1] / control_diag, chebyshev(chebyshev(vector[2], damping), damping))
    zeros = jnp.zeros_like(rhs_state)
    lanczos_old = (zeros, zeros, zeros)
    lanczos_now = (rhs_state, rhs_control, rhs_adjoint)
    precond = precondition(lanczos_now)
    gamma_now = jnp.sqrt(local_inner(precond, lanczos_now))
    gamma_old = jnp.float32(1.0)
    eta_value = gamma_now
    cos_old = jnp.float32(1.0)
    cos_now = jnp.float32(1.0)
    sin_old = jnp.float32(0.0)
    sin_now = jnp.float32(0.0)
    search_old = (zeros, zeros, zeros)
    search_now = (zeros, zeros, zeros)
    iterate = (zeros, zeros, zeros)
    for iteration in range(ITERS):
        precond_now = tuple((f / gamma_now for f in precond))
        image_now = apply_kkt(precond_now)
        delta_now = local_inner(image_now, precond_now)
        coef_one = delta_now / gamma_now
        coef_two = gamma_now / gamma_old
        lanczos_next = tuple((a - coef_one * b - coef_two * c for a, b, c in zip(image_now, lanczos_now, lanczos_old)))
        precond = precondition(lanczos_next)
        gamma_next = jnp.sqrt(local_inner(precond, lanczos_next))
        alpha_zero = cos_now * delta_now - cos_old * sin_now * gamma_now
        alpha_one = jnp.sqrt(alpha_zero * alpha_zero + gamma_next * gamma_next)
        alpha_two = sin_now * delta_now + cos_old * cos_now * gamma_now
        alpha_three = sin_old * gamma_now
        cos_new = alpha_zero / alpha_one
        sin_new = gamma_next / alpha_one
        search_new = tuple(((p - alpha_three * a - alpha_two * b) / alpha_one for p, a, b in zip(precond_now, search_old, search_now)))
        iterate = tuple((i + cos_new * eta_value * s for i, s in zip(iterate, search_new)))
        eta_value = -sin_new * eta_value
        cos_old, cos_now, sin_old, sin_now = (cos_now, cos_new, sin_now, sin_new)
        search_old, search_now = (search_now, search_new)
        lanczos_old, lanczos_now = (lanczos_now, lanczos_next)
        gamma_old, gamma_now = (gamma_now, gamma_next)
    return (iterate[0], iterate[1], iterate[2])
```

```python
import functools

import jax
import jax.numpy as jnp
from jax import lax
from jax.experimental import pallas as pl
from jax.experimental.pallas import tpu as pltpu
from jax.sharding import PartitionSpec as P

REGULAR = 0.01
CENTRE = 8.0
HALF = 7.5
STRETCH = CENTRE / HALF
Q0 = 1.0 / STRETCH
Q1 = 1.0 / (2.0 * STRETCH - Q0)
Q2 = 1.0 / (2.0 * STRETCH - Q1)
A1, B1 = Q1 * Q0, 2.0 * Q1 / HALF
A2, B2 = Q2 * Q1, 2.0 * Q2 / HALF
K1 = 1.0 + A1 + B1 * (CENTRE - 6.0)
K2 = 1.0 + A2 - 6.0 * B2
KR = B2 * CENTRE - A2
INV = 1.0 / CENTRE
INV2 = INV * INV

C1, V1A, Y1, QC, U1, YQ, Y1B, UQ, P1, YQB, QA, P2, RC, YR = range(14)
FIELDS = 14
LANES = 128
SUB = 8
RIGHT, LEFT, UP, DOWN = range(4)
MESH = pl.DeviceIdType.MESH


def kernel(
    nx,
    ny,
    nz,
    va_in,
    vb_in,
    vc_in,
    bar_in,
    act_in,
    out_a,
    out_b,
    out_c,
    raw,
    raw_act,
    fld,
    aux,
    res,
    ysend,
    yhalo,
    ar1,
    ar2,
    in_sem,
    out_sem,
    send_sem,
    recv_sem,
    ar_send,
    ar_recv,
):
    gx, gy = lax.axis_index("gx"), lax.axis_index("gy")
    mx, my = lax.axis_size("gx"), lax.axis_size("gy")
    nt = ny // SUB
    halves = nz // LANES
    right, left = lax.rem(gx + 1, mx), lax.rem(gx + mx - 1, mx)

    inputs = ((vc_in, raw.at[0]), (va_in, raw.at[1]), (act_in, raw_act), (bar_in, raw.at[2]), (vb_in, raw.at[3]))
    loads = [
        [
            pltpu.make_async_copy(src.at[:, :, pl.ds(h * LANES, LANES)], dst.at[h], in_sem.at[i, h])
            for h in range(halves)
        ]
        for i, (src, dst) in enumerate(inputs)
    ]
    for load in loads:
        for part in load:
            part.start()

    def wait_load(i):
        for part in loads[i]:
            part.wait()

    barrier = pltpu.get_barrier_semaphore()

    def greet_gy(k, carry):
        pl.semaphore_signal(barrier, inc=1, device_id=(gx, lax.rem(gy + k, my)), device_id_type=MESH)
        return carry

    def greet_gx(k, carry):
        pl.semaphore_signal(barrier, inc=1, device_id=(lax.rem(gx + k, mx), gy), device_id_type=MESH)
        return carry

    lax.fori_loop(1, my, greet_gy, 0)
    lax.fori_loop(1, mx, greet_gx, 0)

    @pl.when(gy == 0)
    def _():
        for f in range(FIELDS):
            yhalo[f, 0] = jnp.zeros((nx, 1, nz), jnp.float32)

    @pl.when(gy == my - 1)
    def _():
        for f in range(FIELDS):
            yhalo[f, 1] = jnp.zeros((nx, 1, nz), jnp.float32)

    lane = lax.broadcasted_iota(jnp.int32, (SUB, LANES), 1)
    sub = lax.broadcasted_iota(jnp.int32, (SUB, LANES), 0)
    first_lane, last_lane = lane == 0, lane == LANES - 1
    first_sub, last_sub = sub == 0, sub == SUB - 1
    zero = jnp.zeros((SUB, LANES), jnp.float32)

    def span(h):
        return pl.ds(h * LANES, LANES)

    def copy_to(f, way):
        if way == RIGHT:
            src, dst, device = fld.at[f, nx], fld.at[f, 0], (right, gy)
        elif way == LEFT:
            src, dst, device = fld.at[f, 1], fld.at[f, nx + 1], (left, gy)
        elif way == UP:
            src, dst, device = ysend.at[f, 1], yhalo.at[f, 0], (gx, gy + 1)
        else:
            src, dst, device = ysend.at[f, 0], yhalo.at[f, 1], (gx, gy - 1)
        return pltpu.make_async_remote_copy(
            src_ref=src,
            dst_ref=dst,
            send_sem=send_sem.at[f, way],
            recv_sem=recv_sem.at[f, way],
            device_id=device,
            device_id_type=MESH,
        )

    def send_x(f):
        copy_to(f, RIGHT).start()
        copy_to(f, LEFT).start()

    def send_y(f):
        @pl.when(gy < my - 1)
        def _():
            copy_to(f, UP).start()

        @pl.when(gy > 0)
        def _():
            copy_to(f, DOWN).start()

    def wait_halo(f):
        copy_to(f, RIGHT).wait_recv()
        copy_to(f, LEFT).wait_recv()

        @pl.when(gy > 0)
        def _():
            copy_to(f, UP).wait_recv()

        @pl.when(gy < my - 1)
        def _():
            copy_to(f, DOWN).wait_recv()

    def wait_sent(f):
        copy_to(f, RIGHT).wait_send()
        copy_to(f, LEFT).wait_send()

        @pl.when(gy < my - 1)
        def _():
            copy_to(f, UP).wait_send()

        @pl.when(gy > 0)
        def _():
            copy_to(f, DOWN).wait_send()

    def put(f, x, t, h, value):
        fld[f, x + 1, t, :, span(h)] = value
        if t == 0:
            ysend[f, 0, x, :, span(h)] = value[0:1]
        if t == nt - 1:
            ysend[f, 1, x, :, span(h)] = value[SUB - 1 : SUB]

    def plane_sums(f, x):
        centre = [[fld[f, x + 1, t, :, span(h)] for h in range(halves)] for t in range(nt)]
        low = [yhalo[f, 0, x, :, span(h)] for h in range(halves)]
        high = [yhalo[f, 1, x, :, span(h)] for h in range(halves)]
        for t in range(nt):
            up = [pltpu.roll(v, 1, 1) for v in centre[t]]
            down = [pltpu.roll(v, LANES - 1, 1) for v in centre[t]]
            for h in range(halves):
                if t > 0:
                    before = centre[t - 1][h]
                else:
                    before = jnp.where(first_sub, low[h], pltpu.roll(centre[nt - 1][h], 1, 0))
                if t < nt - 1:
                    after = centre[t + 1][h]
                else:
                    after = jnp.where(last_sub, high[h], pltpu.roll(centre[0][h], SUB - 1, 0))
                below = jnp.where(first_lane, up[h - 1] if h > 0 else zero, up[h])
                above = jnp.where(last_lane, down[h + 1] if h < halves - 1 else zero, down[h])
                sides = fld[f, x, t, :, span(h)] + fld[f, x + 2, t, :, span(h)]
                yield t, h, centre[t][h], sides + (before + after) + (below + above)

    def stage(f_in, f_out, make, accs=()):
        def plane(x, accs):
            for t, h, v, total in plane_sums(f_in, x):
                value, terms = make(x, t, h, v, total)
                if f_out is not None:
                    put(f_out, x, t, h, value)
                accs = tuple(a + b for a, b in zip(accs, terms))
            return accs

        wait_halo(f_in)
        accs = lax.fori_loop(0, 2, lambda k, a: plane(k * (nx - 1), a), accs)
        if f_out is not None:
            send_x(f_out)
        accs = lax.fori_loop(1, nx - 1, plane, accs)
        if f_out is not None:
            send_y(f_out)
        return accs

    E1, E2, OPEN, ICD, VB = range(5)

    def at(f, x, t, h):
        return fld[f, x + 1, t, :, span(h)]

    def also(i, x, t, h):
        return aux[i, x, t, :, span(h)]

    def first_half(x, t, h, v, total):
        return also(E1, x, t, h) * v + B1 * total, ()

    def second_half(f_rhs):
        def make(x, t, h, v, total):
            return also(E2, x, t, h) * v + KR * at(f_rhs, x, t, h) + B2 * total, ()

        return make

    def strided(ref, x, t, h):
        return ref[h, x, pl.ds(t, SUB, stride=nt), :]

    def convert(i, f):
        def plane(x, carry):
            for t in range(nt):
                for h in range(halves):
                    put(f, x, t, h, strided(raw.at[i], x, t, h))
            return carry

        lax.fori_loop(0, nx, plane, 0)

    wait_load(0)
    convert(0, C1)
    wait_load(1)
    convert(1, V1A)
    pl.semaphore_wait(barrier, mx + my - 2)
    for f in (C1, V1A):
        send_x(f)
        send_y(f)
    for i in (2, 3, 4):
        wait_load(i)

    def prepare(x, acc):
        for t in range(nt):
            for h in range(halves):
                fixed = strided(raw_act, x, t, h).astype(jnp.float32)
                opened = 1.0 - fixed
                root = lax.rsqrt(REGULAR + strided(raw.at[2], x, t, h))
                damping = opened * root
                icd = damping * root + fixed
                vb = strided(raw.at[3], x, t, h)
                va = at(V1A, x, t, h)
                aux[E1, x, t, :, span(h)] = K1 - B1 * damping
                aux[E2, x, t, :, span(h)] = K2 - B2 * damping
                aux[OPEN, x, t, :, span(h)] = opened
                aux[ICD, x, t, :, span(h)] = icd
                aux[VB, x, t, :, span(h)] = vb
                acc = acc + (va * va + vb * vb * icd)
        return acc

    sum_ab = lax.fori_loop(0, nx, prepare, zero)

    def ar_copy(buf, i, phase, me, device):
        return pltpu.make_async_remote_copy(
            src_ref=buf.at[i, me],
            dst_ref=buf.at[i, me],
            send_sem=ar_send.at[i, phase],
            recv_sem=ar_recv.at[i, phase],
            device_id=device,
            device_id_type=MESH,
        )

    def ar_rows(i, rows):
        full = zero
        for k, row in enumerate(rows):
            full = jnp.where(sub == k, jnp.sum(row, axis=0, keepdims=True), full)
        ar1[i, gy] = full

        def go(k, carry):
            ar_copy(ar1, i, 0, gy, (gx, lax.rem(gy + k, my))).start()
            return carry

        lax.fori_loop(1, my, go, 0)

    def ar_wait(buf, i, phase, count, sem):
        whole = buf.at[i, pl.ds(0, count - 1)]
        pltpu.make_async_copy(whole, whole, sem.at[i, phase]).wait()

    def ar_middle(i):
        ar_wait(ar1, i, 0, my, ar_recv)
        full = ar1[i, 0]
        for k in range(1, my):
            full = full + ar1[i, k]
        ar2[i, gx] = full

        def go(k, carry):
            ar_copy(ar2, i, 1, gx, (lax.rem(gx + k, mx), gy)).start()
            return carry

        lax.fori_loop(1, mx, go, 0)

    def ar_end(i, count):
        ar_wait(ar2, i, 1, mx, ar_recv)
        full = ar2[i, 0]
        for k in range(1, mx):
            full = full + ar2[i, k]
        full = jnp.sum(full, axis=1, keepdims=True)
        return [jnp.broadcast_to(full[k : k + 1], (SUB, LANES)) for k in range(count)]

    def ar_sent(i):
        ar_wait(ar1, i, 0, my, ar_send)
        ar_wait(ar2, i, 1, mx, ar_send)

    def state_image(x, t, h, v, total):
        pb = also(VB, x, t, h) * also(ICD, x, t, h)
        return 6.0 * v - total - also(OPEN, x, t, h) * pb, ()

    def square_out(make):
        def made(x, t, h, v, total):
            value, _ = make(x, t, h, v, total)
            return value, (value * value,)

        return made

    stage(C1, Y1, first_half)
    stage(V1A, QC, state_image)
    (sum_u,) = stage(Y1, U1, square_out(second_half(C1)), (zero,))
    stage(QC, YQ, first_half)
    stage(U1, Y1B, first_half)
    stage(YQ, UQ, second_half(QC))

    def last_half(x, t, h, v, total):
        value, _ = second_half(U1)(x, t, h, v, total)
        return value, (value * at(QC, x, t, h),)

    (sum_qp,) = stage(Y1B, P1, last_half, (zero,))
    ar_rows(0, [sum_ab + INV2 * sum_u, sum_ab + (2.0 * INV2) * sum_qp])
    stage(UQ, YQB, first_half)
    ar_middle(0)

    def add_image(x, t, h, v, total):
        return at(V1A, x, t, h) + INV2 * (6.0 * v - total), ()

    stage(P1, QA, add_image)
    stage(YQB, P2, second_half(UQ))
    m0, m1 = ar_end(0, 2)
    shift = m1 / m0

    def adjoint_image(x, t, h, v, total):
        icd = also(ICD, x, t, h)
        part = also(OPEN, x, t, h) * icd * (also(VB, x, t, h) - INV2 * at(P1, x, t, h))
        return 6.0 * v - total - part - shift * at(QC, x, t, h), ()

    stage(QA, RC, adjoint_image)

    ZA, ZB, ZC = range(3)

    def close(x, t, h, v, total):
        va, qa, p1 = at(V1A, x, t, h), at(QA, x, t, h), at(P1, x, t, h)
        icd, opened, vb = also(ICD, x, t, h), also(OPEN, x, t, h), also(VB, x, t, h)
        za = qa - shift * va
        ra = za + INV2 * (6.0 * v - total) - shift * (qa - va)
        v2b = (1.0 - shift) * vb - opened * (INV2 * p1)
        zb = v2b * icd
        zc = INV2 * (v - shift * p1)
        rb = v2b - opened * zc
        u2 = at(UQ, x, t, h) - shift * at(U1, x, t, h)
        res[ZA, x, t, :, span(h)] = za
        res[ZB, x, t, :, span(h)] = zb
        res[ZC, x, t, :, span(h)] = zc
        base = za * za + zb * v2b
        return None, (
            base + INV2 * (u2 * u2),
            base + 2.0 * (at(RC, x, t, h) * zc),
            ra * ra + rb * rb * icd,
        )

    sums = stage(P2, None, close, (zero, zero, zero))
    stage(RC, YR, first_half)

    (sum_r,) = stage(YR, None, square_out(second_half(RC)), (zero,))
    ar_rows(1, [sums[0], sums[1], sums[2] + INV2 * sum_r])
    ar_middle(1)
    n2, top, m4 = ar_end(1, 3)

    d2 = top / n2
    g2sq = n2 / m0
    g2 = jnp.sqrt(g2sq)
    g3sq = jnp.maximum(m4 / n2 - d2 * d2 - g2sq, 0.0)
    a1 = jnp.sqrt(shift * shift + g2sq)
    c2, s2 = shift / a1, g2 / a1
    b0 = c2 * d2 - s2 * g2
    b1 = jnp.sqrt(b0 * b0 + g3sq)
    b2 = s2 * d2 + c2 * g2
    c3 = b0 / b1
    on_p = (c2 + c3 * s2 * b2 / b1) / a1
    on_z = -c3 / (b1 * a1)

    def finish(x, carry):
        for t in range(nt):
            for h in range(halves):
                where = (h, x, pl.ds(t, SUB, stride=nt))
                pb = also(VB, x, t, h) * also(ICD, x, t, h)
                raw[(0,) + where] = on_p * at(V1A, x, t, h) + on_z * res[ZA, x, t, :, span(h)]
                raw[(1,) + where] = on_p * pb + on_z * res[ZB, x, t, :, span(h)]
                raw[(2,) + where] = (INV2 * on_p) * at(P1, x, t, h) + on_z * res[ZC, x, t, :, span(h)]
        return carry

    parts = 4
    size = nx // parts
    stores = []
    for p in range(parts):
        lax.fori_loop(p * size, (p + 1) * size, finish, 0)
        for i, out in enumerate((out_a, out_b, out_c)):
            rows = pl.ds(p * size, size)
            for h in range(halves):
                store = pltpu.make_async_copy(
                    raw.at[i, h, rows], out.at[rows, :, pl.ds(h * LANES, LANES)], out_sem.at[i, p, h]
                )
                store.start()
                stores.append(store)
    for f in range(FIELDS):
        wait_sent(f)
    ar_sent(0)
    ar_sent(1)
    for store in stores:
        store.wait()


def shards(va, vb, vc, barrier, active):
    nx, ny, nz = va.shape
    mx, my = lax.axis_size("gx"), lax.axis_size("gy")
    f32 = jnp.float32
    nt = ny // SUB
    hbm = pl.BlockSpec(memory_space=pl.ANY)
    out = jax.ShapeDtypeStruct(va.shape, f32)
    return pl.pallas_call(
        functools.partial(kernel, nx, ny, nz),
        out_shape=(out, out, out),
        in_specs=[hbm] * 5,
        out_specs=(hbm, hbm, hbm),
        scratch_shapes=[
            pltpu.VMEM((4, nz // LANES, nx, ny, LANES), f32),
            pltpu.VMEM((nz // LANES, nx, ny, LANES), jnp.int32),
            pltpu.VMEM((FIELDS, nx + 2, nt, SUB, nz), f32),
            pltpu.VMEM((5, nx, nt, SUB, nz), f32),
            pltpu.VMEM((3, nx, nt, SUB, nz), f32),
            pltpu.VMEM((FIELDS, 2, nx, 1, nz), f32),
            pltpu.VMEM((FIELDS, 2, nx, 1, nz), f32),
            pltpu.VMEM((2, my, SUB, LANES), f32),
            pltpu.VMEM((2, mx, SUB, LANES), f32),
            pltpu.SemaphoreType.DMA((5, nz // LANES)),
            pltpu.SemaphoreType.DMA((3, 4, nz // LANES)),
            pltpu.SemaphoreType.DMA((FIELDS, 4)),
            pltpu.SemaphoreType.DMA((FIELDS, 4)),
            pltpu.SemaphoreType.DMA((2, 2)),
            pltpu.SemaphoreType.DMA((2, 2)),
        ],
        compiler_params=pltpu.CompilerParams(
            collective_id=0, has_side_effects=True, vmem_limit_bytes=48 * 1024 * 1024
        ),
    )(va, vb, vc, barrier, active)


def solution(mesh):
    placed = P("gx", "gy", None)
    return jax.shard_map(
        shards,
        mesh=mesh,
        in_specs=(placed,) * 5,
        out_specs=(placed,) * 3,
        check_vma=False,
    )
```

```python
import functools

import jax
import jax.numpy as jnp
from jax import lax
from jax.experimental import pallas as pl
from jax.experimental.pallas import tpu as pltpu
from jax.sharding import PartitionSpec as P

REGULAR = 0.01
CENTRE = 8.0
HALF = 7.5
STRETCH = CENTRE / HALF
Q0 = 1.0 / STRETCH
Q1 = 1.0 / (2.0 * STRETCH - Q0)
Q2 = 1.0 / (2.0 * STRETCH - Q1)
A1, B1 = Q1 * Q0, 2.0 * Q1 / HALF
A2, B2 = Q2 * Q1, 2.0 * Q2 / HALF
K1 = 1.0 + A1 + B1 * (CENTRE - 6.0)
K2 = 1.0 + A2 - 6.0 * B2
KR = B2 * CENTRE - A2
INV = 1.0 / CENTRE
INV2 = INV * INV

LANES = 128
SUB = 8
DEEP = 4
STEPS = 2
MESH = pl.DeviceIdType.MESH
WAYS = ((1, 0), (-1, 0), (0, 1), (0, -1), (1, 1), (-1, 1), (1, -1), (-1, -1))
DEEP_FIELDS = ("c1", "damp", "qc", "p1")
FLAT_FIELDS = ("v1a", "p2")
LOCAL_FIELDS = ("tmp", "u1", "uq", "kp", "rc", "e1", "e2")
OWN_FIELDS = ("open", "icd", "vb", "za", "zb", "zc")


def scratch(nx, ny, nz, mx, my):
    f32 = jnp.float32
    nt, halves = ny // SUB, nz // LANES
    shapes = {
        "raw": pltpu.VMEM((4, halves, nx, ny, LANES), f32),
        "raw_act": pltpu.VMEM((halves, nx, ny, LANES), jnp.int32),
        "ar1": pltpu.VMEM((2, my, SUB, LANES), f32),
        "ar2": pltpu.VMEM((2, mx, SUB, LANES), f32),
        "in_sem": pltpu.SemaphoreType.DMA((5, halves)),
        "out_sem": pltpu.SemaphoreType.DMA((3, 4, halves)),
        "ar_send": pltpu.SemaphoreType.DMA((2, 2)),
        "ar_recv": pltpu.SemaphoreType.DMA((2, 2)),
    }
    shapes["band"] = pltpu.VMEM((nz, nz), jnp.bfloat16)
    for name in DEEP_FIELDS + LOCAL_FIELDS:
        shapes[name] = pltpu.VMEM((nx + 2 * DEEP, nt, SUB, nz), f32)
        shapes[name + "_rim"] = pltpu.VMEM((nx + 2 * DEEP, SUB, nz), f32)
    for name in FLAT_FIELDS:
        shapes[name] = pltpu.VMEM((nx + 2, nt, SUB, nz), f32)
    for name in OWN_FIELDS:
        shapes[name] = pltpu.VMEM((nx, nt, SUB, nz), f32)
    for name in DEEP_FIELDS + FLAT_FIELDS:
        rows, pad = (DEEP, DEEP) if name in DEEP_FIELDS else (1, 0)
        for side in ("_low", "_high"):
            shapes[name + side] = pltpu.VMEM((nx + 2 * pad, rows, nz), f32)
        for side in ("_down", "_up"):
            shapes[name + side] = pltpu.VMEM((nx, rows, nz), f32)
        shapes[name + "_send"] = pltpu.SemaphoreType.DMA((8,))
        shapes[name + "_recv"] = pltpu.SemaphoreType.DMA((8,))
    return shapes


def kernel(nx, ny, nz, names, va_in, vb_in, vc_in, bar_in, act_in, out_a, out_b, out_c, *scratch_refs):
    ref = dict(zip(names, scratch_refs))
    raw, raw_act = ref["raw"], ref["raw_act"]
    gx, gy = lax.axis_index("gx"), lax.axis_index("gy")
    mx, my = lax.axis_size("gx"), lax.axis_size("gy")
    nt = ny // SUB
    halves = nz // LANES

    inputs = ((vc_in, raw.at[0]), (va_in, raw.at[1]), (act_in, raw_act), (bar_in, raw.at[2]), (vb_in, raw.at[3]))
    loads = [
        [
            pltpu.make_async_copy(src.at[:, :, pl.ds(h * LANES, LANES)], dst.at[h], ref["in_sem"].at[i, h])
            for h in range(halves)
        ]
        for i, (src, dst) in enumerate(inputs)
    ]
    for load in loads:
        for part in load:
            part.start()

    def wait_load(i):
        for part in loads[i]:
            part.wait()

    barrier = pltpu.get_barrier_semaphore()

    def greet(sx, sy):
        device = (lax.rem(gx + sx, mx), lax.rem(gy + sy, my))
        pl.semaphore_signal(barrier, inc=1, device_id=device, device_id_type=MESH)

    def greet_gy(k, carry):
        greet(0, k)
        return carry

    def greet_gx(k, carry):
        greet(k, 0)
        return carry

    lax.fori_loop(1, my, greet_gy, 0)
    lax.fori_loop(1, mx, greet_gx, 0)
    for sx in (1, mx - 1):
        for sy in (1, my - 1):
            greet(sx, sy)

    def clear(side):
        for name in DEEP_FIELDS + FLAT_FIELDS:
            edge = ref[name + side]
            edge[...] = jnp.zeros(edge.shape, jnp.float32)

    pl.when(gy == 0)(lambda: clear("_low"))
    pl.when(gy == my - 1)(lambda: clear("_high"))

    sub = lax.broadcasted_iota(jnp.int32, (SUB, LANES), 0)
    zero = jnp.zeros((SUB, LANES), jnp.float32)
    inside = jnp.where(sub < DEEP, gy, my - 1 - gy) > 0

    def span(h):
        return pl.ds(h * LANES, LANES)

    def copy_to(name, way):
        sx, sy = WAYS[way]
        deep = name in DEEP_FIELDS
        pad = DEEP if deep else 1
        if sy == 0:
            src, dst = (nx, 0) if sx > 0 else (pad, nx + pad)
            src, dst = ref[name].at[pl.ds(src, pad)], ref[name].at[pl.ds(dst, pad)]
        else:
            src, dst = ref[name + ("_up" if sy > 0 else "_down")], ref[name + ("_low" if sy > 0 else "_high")]
            if sx == 0:
                dst = dst.at[pl.ds(DEEP if deep else 0, nx)]
            else:
                src = src.at[pl.ds(nx - DEEP if sx > 0 else 0, DEEP)]
                dst = dst.at[pl.ds(0 if sx > 0 else nx + DEEP, DEEP)]
        return pltpu.make_async_remote_copy(
            src_ref=src,
            dst_ref=dst,
            send_sem=ref[name + "_send"].at[way],
            recv_sem=ref[name + "_recv"].at[way],
            device_id=(lax.rem(gx + mx + sx, mx), gy + sy),
            device_id_type=MESH,
        )

    def send_x(name):
        copy_to(name, 0).start()
        copy_to(name, 1).start()

    def along_y(name, act, taking):
        for step in (1, -1):

            @pl.when(gy < my - 1 if (step > 0) != taking else gy > 0)
            def _():
                for way, (_, sy) in enumerate(WAYS):
                    if sy == step and (name in DEEP_FIELDS or way < 4):
                        act(copy_to(name, way))

    def send_y(name):
        along_y(name, lambda copy: copy.start(), False)

    def wait_halo(name):
        copy_to(name, 0).wait_recv()
        copy_to(name, 1).wait_recv()
        along_y(name, lambda copy: copy.wait_recv(), True)

    def wait_sent(name):
        copy_to(name, 0).wait_send()
        copy_to(name, 1).wait_send()
        along_y(name, lambda copy: copy.wait_send(), False)

    def pad_of(name):
        return DEEP if name in DEEP_FIELDS + LOCAL_FIELDS else 1 if name in FLAT_FIELDS else 0

    def at(name, x, t, h):
        if t == nt:
            return ref[name + "_rim"][x + DEEP, :, span(h)]
        return ref[name][x + pad_of(name), t, :, span(h)]

    def put(name, x, t, h, value, pack=True):
        if t == nt:
            ref[name + "_rim"][x + DEEP, :, span(h)] = value
            return
        ref[name][x + pad_of(name), t, :, span(h)] = value
        if not pack:
            return
        if name in DEEP_FIELDS:
            if t < DEEP:
                ref[name + "_down"][x, t : t + 1, span(h)] = value[0:1]
            if t >= nt - DEEP:
                ref[name + "_up"][x, t - nt + DEEP : t - nt + DEEP + 1, span(h)] = value[SUB - 1 : SUB]
        elif name in FLAT_FIELDS:
            if t == 0:
                ref[name + "_down"][x, :, span(h)] = value[0:1]
            if t == nt - 1:
                ref[name + "_up"][x, :, span(h)] = value[SUB - 1 : SUB]

    def over(first, last, plane, carry=0):
        return lax.fori_loop(0, last - first, lambda k, c: plane(k + first, c), carry)

    def merge(name):
        def plane(x, carry):
            for h in range(halves):
                low, high = ref[name + "_low"][x, :, span(h)], ref[name + "_high"][x, :, span(h)]
                ref[name + "_rim"][x, :, span(h)] = jnp.concatenate([low, high], axis=0)
            return carry

        over(0, nx + 2 * DEEP, plane)

    rows = lax.broadcasted_iota(jnp.int32, (nz, nz), 0)
    columns = lax.broadcasted_iota(jnp.int32, (nz, nz), 1)
    ref["band"][...] = jnp.where(jnp.abs(rows - columns) == 1, 1.0, 0.0).astype(jnp.bfloat16)

    def along_z(values):
        top = values.astype(jnp.bfloat16)
        rest = (values - top.astype(jnp.float32)).astype(jnp.bfloat16)
        band = ref["band"][...]
        return jnp.dot(top, band, preferred_element_type=jnp.float32) + jnp.dot(
            rest, band, preferred_element_type=jnp.float32
        )

    def plane_sums(name, x, count, rim):
        flat = name in FLAT_FIELDS
        body = ref[name][pl.ds(x + pad_of(name), count)].reshape(count * ny, nz)
        z_body = along_z(body)
        if rim:
            z_rim = along_z(ref[name + "_rim"][pl.ds(x + DEEP, count)].reshape(count * SUB, nz))
        found = []
        for c in range(count):
            for t in range(nt + 1 if rim else nt):
                for h in range(halves):
                    v = at(name, x + c, t, h)
                    first, last = at(name, x + c, 0, h), at(name, x + c, nt - 1, h)
                    if t == nt:
                        before = jnp.where(sub == DEEP, pltpu.roll(last, DEEP + 1, 0), pltpu.roll(v, 1, 0))
                        after = jnp.where(sub == DEEP - 1, pltpu.roll(first, DEEP - 1, 0), pltpu.roll(v, SUB - 1, 0))
                        along = z_rim[c * SUB : (c + 1) * SUB, h * LANES : (h + 1) * LANES]
                    else:
                        if t > 0:
                            before = at(name, x + c, t - 1, h)
                        else:
                            if flat:
                                edge = ref[name + "_low"][x + c, :, span(h)]
                            else:
                                edge = pltpu.roll(at(name, x + c, nt, h), DEEP + 1, 0)
                            before = jnp.where(sub == 0, edge, pltpu.roll(last, 1, 0))
                        if t < nt - 1:
                            after = at(name, x + c, t + 1, h)
                        else:
                            if flat:
                                edge = ref[name + "_high"][x + c, :, span(h)]
                            else:
                                edge = pltpu.roll(at(name, x + c, nt, h), DEEP - 1, 0)
                            after = jnp.where(sub == SUB - 1, edge, pltpu.roll(first, SUB - 1, 0))
                        row = (c * nt + t) * SUB
                        along = z_body[row : row + SUB, h * LANES : (h + 1) * LANES]
                    sides = at(name, x + c - 1, t, h) + at(name, x + c + 1, t, h)
                    found.append((x + c, t, h, v, sides + (before + after) + along))
        return found

    def stage(f_in, f_out, make, width=0, accs=()):
        rim = width > 0
        f_outs = f_out if isinstance(f_out, tuple) else (f_out,) if f_out else ()

        def planes(first, count, accs):
            done = []
            for x, t, h, v, total in plane_sums(f_in, first, count, rim):
                value, terms = make(x, t, h, v, total)
                if t == nt:
                    value = jnp.where(inside, value, 0.0)
                else:
                    accs = tuple(a + b for a, b in zip(accs, terms))
                done.append((x, t, h, value if isinstance(value, tuple) else (value,)))
            for x, t, h, values in done:
                for name, value in zip(f_outs, values):
                    put(name, x, t, h, value)
            return accs

        if f_out in DEEP_FIELDS + FLAT_FIELDS:
            depth = DEEP
            accs = lax.fori_loop(0, 2, lambda k, a: planes(k * (nx - depth), depth, a), accs)
            send_x(f_out)
            inner = (nx - 2 * depth) // 2
            accs = lax.fori_loop(0, 2, lambda k, a: planes(depth + k * inner, inner, a), accs)
            send_y(f_out)
            return accs
        steps = STEPS
        count = (nx + 2 * width) // steps
        return lax.fori_loop(0, steps, lambda k, a: planes(k * count - width, count, a), accs)

    def first_half(x, t, h, v, total):
        return at("e1", x, t, h) * v + B1 * total, ()

    def second_half(rhs):
        def make(x, t, h, v, total):
            return at("e2", x, t, h) * v + KR * at(rhs, x, t, h) + B2 * total, ()

        return make

    def strided(buf, x, t, h):
        return buf[h, x, pl.ds(t, SUB, stride=nt), :]

    def convert(i, name):
        def plane(x, carry):
            values = [(t, h, strided(raw.at[i], x, t, h)) for t in range(nt) for h in range(halves)]
            for t, h, value in values:
                put(name, x, t, h, value)
            return carry

        over(0, nx, plane)

    wait_load(1)
    convert(1, "v1a")
    wait_load(0)
    convert(0, "c1")
    pl.semaphore_wait(barrier, mx + my + 2)
    for name in ("v1a", "c1"):
        send_x(name)
        send_y(name)
    for i in (2, 3, 4):
        wait_load(i)

    def coefficients(x, t, h, damping):
        put("e1", x, t, h, K1 - B1 * damping)
        put("e2", x, t, h, K2 - B2 * damping)

    def prepare(x, acc):
        done = []
        for t in range(nt):
            for h in range(halves):
                fixed = strided(raw_act, x, t, h).astype(jnp.float32)
                opened = 1.0 - fixed
                root = lax.rsqrt(REGULAR + strided(raw.at[2], x, t, h))
                damping = opened * root
                icd = damping * root + fixed
                vb = strided(raw.at[3], x, t, h)
                va = at("v1a", x, t, h)
                acc = acc + (va * va + vb * vb * icd)
                done.append((t, h, damping, opened, icd, vb))
        for t, h, damping, opened, icd, vb in done:
            put("damp", x, t, h, damping)
            put("open", x, t, h, opened)
            put("icd", x, t, h, icd)
            put("vb", x, t, h, vb)
            coefficients(x, t, h, damping)
        return acc

    sum_ab = over(0, nx, prepare, zero)
    send_x("damp")
    send_y("damp")

    def rim_coefficients():
        merge("damp")

        def rim(x, carry):
            for h in range(halves):
                coefficients(x, nt, h, at("damp", x, nt, h))
            return carry

        def outside(x, carry):
            for t in range(nt):
                for h in range(halves):
                    coefficients(x, t, h, at("damp", x, t, h))
            return carry

        over(-DEEP, nx + DEEP, rim)
        over(1 - DEEP, 0, outside)
        over(nx, nx + DEEP - 1, outside)

    ar1, ar2, ar_send, ar_recv = ref["ar1"], ref["ar2"], ref["ar_send"], ref["ar_recv"]

    def ar_copy(buf, i, phase, me, device):
        return pltpu.make_async_remote_copy(
            src_ref=buf.at[i, me],
            dst_ref=buf.at[i, me],
            send_sem=ar_send.at[i, phase],
            recv_sem=ar_recv.at[i, phase],
            device_id=device,
            device_id_type=MESH,
        )

    def ar_rows(i, rows):
        full = zero
        for k, row in enumerate(rows):
            full = jnp.where(sub == k, jnp.sum(row, axis=0, keepdims=True), full)
        ar1[i, gy] = full

        def go(k, carry):
            ar_copy(ar1, i, 0, gy, (gx, lax.rem(gy + k, my))).start()
            return carry

        lax.fori_loop(1, my, go, 0)

    def ar_wait(buf, i, phase, count, sem):
        whole = buf.at[i, pl.ds(0, count - 1)]
        pltpu.make_async_copy(whole, whole, sem.at[i, phase]).wait()

    def ar_middle(i):
        ar_wait(ar1, i, 0, my, ar_recv)
        full = ar1[i, 0]
        for k in range(1, my):
            full = full + ar1[i, k]
        ar2[i, gx] = full

        def go(k, carry):
            ar_copy(ar2, i, 1, gx, (lax.rem(gx + k, mx), gy)).start()
            return carry

        lax.fori_loop(1, mx, go, 0)

    def ar_end(i, count):
        ar_wait(ar2, i, 1, mx, ar_recv)
        full = ar2[i, 0]
        for k in range(1, mx):
            full = full + ar2[i, k]
        full = jnp.sum(full, axis=1, keepdims=True)
        return [jnp.broadcast_to(full[k : k + 1], (SUB, LANES)) for k in range(count)]

    def ar_sent(i):
        ar_wait(ar1, i, 0, my, ar_send)
        ar_wait(ar2, i, 1, mx, ar_send)

    def square_out(make):
        def made(x, t, h, v, total):
            value, _ = make(x, t, h, v, total)
            return value, (value * value,)

        return made

    def state_image(x, t, h, v, total):
        return 6.0 * v - total - at("open", x, t, h) * (at("vb", x, t, h) * at("icd", x, t, h)), ()

    wait_halo("v1a")
    stage("v1a", "qc", state_image)

    wait_halo("c1")
    merge("c1")
    wait_halo("damp")
    rim_coefficients()
    stage("c1", "tmp", first_half, 3)
    stage("tmp", "u1", second_half("c1"), 2)
    stage("u1", "tmp", first_half, 1)

    def last_half(x, t, h, v, total):
        value, _ = second_half("u1")(x, t, h, v, total)
        u1 = at("u1", x, t, h)
        return value, (u1 * u1, value * at("qc", x, t, h))

    sum_u, sum_qp = stage("tmp", "p1", last_half, 0, (zero, zero))
    ar_rows(0, [sum_ab + INV2 * sum_u, sum_ab + (2.0 * INV2) * sum_qp])

    wait_halo("qc")
    merge("qc")
    stage("qc", "tmp", first_half, 3)
    stage("tmp", "uq", second_half("qc"), 2)
    ar_middle(0)
    stage("uq", "tmp", first_half, 1)
    stage("tmp", "p2", second_half("uq"))

    wait_halo("p1")
    merge("p1")
    stage("p1", "kp", lambda x, t, h, v, total: (6.0 * v - total, ()), 3)
    m0, m1 = ar_end(0, 2)
    shift = m1 / m0

    def adjoint_image(x, t, h, v, total):
        damping = at("damp", x, t, h)
        part = 6.0 * v - total + damping * damping * at("p1", x, t, h)
        return INV2 * part + (1.0 - shift) * at("qc", x, t, h), ()

    stage("kp", "rc", adjoint_image, 2)
    stage("rc", "tmp", first_half, 1)
    (sum_r,) = stage("tmp", None, square_out(second_half("rc")), 0, (zero,))

    def close(x, t, h, v, total):
        va, p1 = at("v1a", x, t, h), at("p1", x, t, h)
        icd, opened, vb = at("icd", x, t, h), at("open", x, t, h), at("vb", x, t, h)
        step = INV2 * at("kp", x, t, h)
        za = (va + step) - shift * va
        ra = za + INV2 * (6.0 * v - total) - shift * step
        v2b = (1.0 - shift) * vb - opened * (INV2 * p1)
        zb = v2b * icd
        zc = INV2 * (v - shift * p1)
        rb = v2b - opened * zc
        u2 = at("uq", x, t, h) - shift * at("u1", x, t, h)
        base = za * za + zb * v2b
        return (za, zb, zc), (
            base + INV2 * (u2 * u2),
            base + 2.0 * (at("rc", x, t, h) * zc),
            ra * ra + rb * rb * icd,
        )

    wait_halo("p2")
    sums = stage("p2", ("za", "zb", "zc"), close, 0, (zero, zero, zero))
    ar_rows(1, [sums[0], sums[1], sums[2] + INV2 * sum_r])
    ar_middle(1)
    n2, top, m4 = ar_end(1, 3)

    d2 = top / n2
    g2sq = n2 / m0
    g2 = jnp.sqrt(g2sq)
    g3sq = jnp.maximum(m4 / n2 - d2 * d2 - g2sq, 0.0)
    a1 = jnp.sqrt(shift * shift + g2sq)
    c2, s2 = shift / a1, g2 / a1
    b0 = c2 * d2 - s2 * g2
    b1 = jnp.sqrt(b0 * b0 + g3sq)
    b2 = s2 * d2 + c2 * g2
    c3 = b0 / b1
    on_p = (c2 + c3 * s2 * b2 / b1) / a1
    on_z = -c3 / (b1 * a1)

    def finish(x, carry):
        done = []
        for t in range(nt):
            for h in range(halves):
                pb = at("vb", x, t, h) * at("icd", x, t, h)
                done.append((0, t, h, on_p * at("v1a", x, t, h) + on_z * at("za", x, t, h)))
                done.append((1, t, h, on_p * pb + on_z * at("zb", x, t, h)))
                done.append((2, t, h, (INV2 * on_p) * at("p1", x, t, h) + on_z * at("zc", x, t, h)))
        for i, t, h, value in done:
            raw[i, h, x, pl.ds(t, SUB, stride=nt), :] = value
        return carry

    parts = 4
    size = nx // parts
    stores = []
    for p in range(parts):
        over(p * size, (p + 1) * size, finish)
        for i, out in enumerate((out_a, out_b, out_c)):
            rows = pl.ds(p * size, size)
            for h in range(halves):
                store = pltpu.make_async_copy(
                    raw.at[i, h, rows], out.at[rows, :, pl.ds(h * LANES, LANES)], ref["out_sem"].at[i, p, h]
                )
                store.start()
                stores.append(store)
    for name in DEEP_FIELDS + FLAT_FIELDS:
        wait_sent(name)
    ar_sent(0)
    ar_sent(1)
    for store in stores:
        store.wait()


def shards(va, vb, vc, barrier, active):
    nx, ny, nz = va.shape
    hbm = pl.BlockSpec(memory_space=pltpu.HBM)
    out = jax.ShapeDtypeStruct(va.shape, jnp.float32)
    shapes = scratch(nx, ny, nz, lax.axis_size("gx"), lax.axis_size("gy"))
    return pl.pallas_call(
        functools.partial(kernel, nx, ny, nz, tuple(shapes)),
        out_shape=(out, out, out),
        in_specs=[hbm] * 5,
        out_specs=(hbm, hbm, hbm),
        scratch_shapes=list(shapes.values()),
        compiler_params=pltpu.CompilerParams(
            collective_id=0, has_side_effects=True, vmem_limit_bytes=54 * 1024 * 1024
        ),
    )(va, vb, vc, barrier, active)


def solution(mesh):
    placed = P("gx", "gy", None)
    return jax.shard_map(
        shards,
        mesh=mesh,
        in_specs=(placed,) * 5,
        out_specs=(placed,) * 3,
        check_vma=False,
    )
```

```python
import functools

import jax
import jax.numpy as jnp
from jax import lax
from jax.experimental import pallas as pl
from jax.experimental.pallas import tpu as pltpu
from jax.sharding import PartitionSpec as P

REGULAR = 0.01
CENTRE = 8.0
HALF = 7.5
STRETCH = CENTRE / HALF
Q0 = 1.0 / STRETCH
Q1 = 1.0 / (2.0 * STRETCH - Q0)
Q2 = 1.0 / (2.0 * STRETCH - Q1)
A1, B1 = Q1 * Q0, 2.0 * Q1 / HALF
A2, B2 = Q2 * Q1, 2.0 * Q2 / HALF
K1 = 1.0 + A1 + B1 * (CENTRE - 6.0)
K2 = 1.0 + A2 - 6.0 * B2
KR = B2 * CENTRE - A2
INV = 1.0 / CENTRE
INV2 = INV * INV

LANES = 128
SUB = 8
DEEP = 4
MESH = pl.DeviceIdType.MESH
WAYS = ((1, 0), (-1, 0), (0, 1), (0, -1), (1, 1), (-1, 1), (1, -1), (-1, -1))
DEEP_FIELDS = ("c1", "damp", "qc", "p1")
FLAT_FIELDS = ("v1a", "p2")
LOCAL_FIELDS = ("half", "half_q", "u1", "uq", "kp", "rc", "e1", "e2")
OWN_FIELDS = ("open", "icd", "vb", "ur", "kp2")
HANDED_ON = ("pa", "pb", "pc", "za", "zb", "zc")


def scratch(nx, ny, nz, mx, my):
    f32 = jnp.float32
    nt, halves = ny // SUB, nz // LANES
    shapes = {
        "raw": pltpu.VMEM((4, halves, nx, ny, LANES), f32),
        "raw_act": pltpu.VMEM((halves, nx, ny, LANES), jnp.int32),
        "ar1": pltpu.VMEM((2, my, SUB, LANES), f32),
        "ar2": pltpu.VMEM((2, mx, SUB, LANES), f32),
        "in_sem": pltpu.SemaphoreType.DMA((5, halves)),
        "ar_send": pltpu.SemaphoreType.DMA((2, 2)),
        "ar_recv": pltpu.SemaphoreType.DMA((2, 2)),
    }
    shapes["band"] = pltpu.VMEM((nz, nz), jnp.bfloat16)
    for name in DEEP_FIELDS + LOCAL_FIELDS:
        shapes[name] = pltpu.VMEM((nx + 2 * DEEP, nt, SUB, nz), f32)
        shapes[name + "_rim"] = pltpu.VMEM((nx + 2 * DEEP, SUB, nz), f32)
    for name in FLAT_FIELDS:
        shapes[name] = pltpu.VMEM((nx + 2, nt, SUB, nz), f32)
    for name in OWN_FIELDS:
        shapes[name] = pltpu.VMEM((nx, nt, SUB, nz), f32)
    for name in DEEP_FIELDS + FLAT_FIELDS:
        rows, pad = (DEEP, DEEP) if name in DEEP_FIELDS else (1, 0)
        for side in ("_low", "_high"):
            shapes[name + side] = pltpu.VMEM((nx + 2 * pad, rows, nz), f32)
        for side in ("_down", "_up"):
            shapes[name + side] = pltpu.VMEM((nx, rows, nz), f32)
        shapes[name + "_send"] = pltpu.SemaphoreType.DMA((8,))
        shapes[name + "_recv"] = pltpu.SemaphoreType.DMA((8,))
    return shapes


def kernel(nx, ny, nz, names, va_in, vb_in, vc_in, bar_in, act_in, *refs):
    ref = dict(zip(HANDED_ON + ("coef",) + names, refs))
    raw, raw_act = ref["raw"], ref["raw_act"]
    gx, gy = lax.axis_index("gx"), lax.axis_index("gy")
    mx, my = lax.axis_size("gx"), lax.axis_size("gy")
    nt = ny // SUB
    halves = nz // LANES

    inputs = ((vc_in, raw.at[0]), (va_in, raw.at[1]), (act_in, raw_act), (bar_in, raw.at[2]), (vb_in, raw.at[3]))
    loads = [
        [
            pltpu.make_async_copy(src.at[:, :, pl.ds(h * LANES, LANES)], dst.at[h], ref["in_sem"].at[i, h])
            for h in range(halves)
        ]
        for i, (src, dst) in enumerate(inputs)
    ]
    for load in loads:
        for part in load:
            part.start()

    def wait_load(i):
        for part in loads[i]:
            part.wait()

    barrier = pltpu.get_barrier_semaphore()

    def greet(sx, sy):
        device = (lax.rem(gx + sx, mx), lax.rem(gy + sy, my))
        pl.semaphore_signal(barrier, inc=1, device_id=device, device_id_type=MESH)

    far_x = sorted(range(1, mx), key=lambda k: abs(2 * k - mx))
    far_y = sorted(range(1, my), key=lambda k: abs(2 * k - my))
    for k in far_x:
        greet(k, 0)
    for sx in (1, mx - 1):
        for sy in (1, my - 1):
            greet(sx, sy)
    for k in far_y:
        greet(0, k)

    def clear(side):
        for name in DEEP_FIELDS + FLAT_FIELDS:
            edge = ref[name + side]
            edge[...] = jnp.zeros(edge.shape, jnp.float32)

    pl.when(gy == 0)(lambda: clear("_low"))
    pl.when(gy == my - 1)(lambda: clear("_high"))

    sub = lax.broadcasted_iota(jnp.int32, (SUB, LANES), 0)
    zero = jnp.zeros((SUB, LANES), jnp.float32)
    inside = jnp.where(sub < DEEP, gy, my - 1 - gy) > 0

    def span(h):
        return pl.ds(h * LANES, LANES)

    def copy_to(name, way):
        sx, sy = WAYS[way]
        deep = name in DEEP_FIELDS
        pad = DEEP if deep else 1
        if sy == 0:
            depth = DEEP - 1 if name == "damp" else pad
            src, dst = (nx - depth, -depth) if sx > 0 else (0, nx)
            src, dst = ref[name].at[pl.ds(src + pad, depth)], ref[name].at[pl.ds(dst + pad, depth)]
        else:
            src, dst = ref[name + ("_up" if sy > 0 else "_down")], ref[name + ("_low" if sy > 0 else "_high")]
            if sx == 0:
                dst = dst.at[pl.ds(DEEP if deep else 0, nx)]
            else:
                count = DEEP - 2 if name == "damp" else DEEP - 1
                src = src.at[pl.ds(nx - count if sx > 0 else 0, count)]
                dst = dst.at[pl.ds(DEEP - count if sx > 0 else nx + DEEP, count)]
        return pltpu.make_async_remote_copy(
            src_ref=src,
            dst_ref=dst,
            send_sem=ref[name + "_send"].at[way],
            recv_sem=ref[name + "_recv"].at[way],
            device_id=(lax.rem(gx + mx + sx, mx), gy + sy),
            device_id_type=MESH,
        )

    def send_x(name):
        copy_to(name, 0).start()
        copy_to(name, 1).start()

    def along_y(name, act, taking, ways):
        for step in (1, -1):

            @pl.when(gy < my - 1 if (step > 0) != taking else gy > 0)
            def _():
                for way in ways:
                    if WAYS[way][1] == step:
                        act(copy_to(name, way))

    def all_ways(name):
        return range(2, 8 if name in DEEP_FIELDS else 4)

    def send_y(name):
        along_y(name, lambda copy: copy.start(), False, all_ways(name))

    def wait_y(name):
        along_y(name, lambda copy: copy.wait_recv(), True, (2, 3))

    def wait_x(name):
        copy_to(name, 0).wait_recv()
        copy_to(name, 1).wait_recv()
        if name in DEEP_FIELDS:
            along_y(name, lambda copy: copy.wait_recv(), True, (4, 5, 6, 7))

    def wait_sent(name):
        copy_to(name, 0).wait_send()
        copy_to(name, 1).wait_send()
        along_y(name, lambda copy: copy.wait_send(), False, all_ways(name))

    def pad_of(name):
        return DEEP if name in DEEP_FIELDS + LOCAL_FIELDS else 1 if name in FLAT_FIELDS else 0

    def at(name, x, t, h):
        if t == nt:
            return ref[name + "_rim"][x + DEEP, :, span(h)]
        return ref[name][x + pad_of(name), t, :, span(h)]

    def put(name, x, t, h, value, pack=True):
        if t == nt:
            ref[name + "_rim"][x + DEEP, :, span(h)] = value
            return
        ref[name][x + pad_of(name), t, :, span(h)] = value
        if not pack:
            return
        if name in DEEP_FIELDS:
            if t < DEEP:
                ref[name + "_down"][x, t : t + 1, span(h)] = value[0:1]
            if t >= nt - DEEP:
                ref[name + "_up"][x, t - nt + DEEP : t - nt + DEEP + 1, span(h)] = value[SUB - 1 : SUB]
        elif name in FLAT_FIELDS:
            if t == 0:
                ref[name + "_down"][x, :, span(h)] = value[0:1]
            if t == nt - 1:
                ref[name + "_up"][x, :, span(h)] = value[SUB - 1 : SUB]

    def over(first, last, plane, carry=0):
        return lax.fori_loop(0, last - first, lambda k, c: plane(k + first, c), carry)

    def merge(name, first, last):
        def plane(x, carry):
            for h in range(halves):
                low, high = ref[name + "_low"][x, :, span(h)], ref[name + "_high"][x, :, span(h)]
                ref[name + "_rim"][x, :, span(h)] = jnp.concatenate([low, high], axis=0)
            return carry

        over(first + DEEP, last + DEEP, plane)

    def merge_inner(name):
        wait_y(name)
        merge(name, 0, nx)

    def merge_outer(name):
        wait_x(name)
        merge(name, -DEEP, 0)
        merge(name, nx, nx + DEEP)

    rows = lax.broadcasted_iota(jnp.int32, (nz, nz), 0)
    columns = lax.broadcasted_iota(jnp.int32, (nz, nz), 1)
    ref["band"][...] = jnp.where(jnp.abs(rows - columns) == 1, 1.0, 0.0).astype(jnp.bfloat16)

    def along_z(values):
        top = values.astype(jnp.bfloat16)
        rest = (values - top.astype(jnp.float32)).astype(jnp.bfloat16)
        band = ref["band"][...]
        return jnp.dot(top, band, preferred_element_type=jnp.float32) + jnp.dot(
            rest, band, preferred_element_type=jnp.float32
        )

    def plane_sums(name, parts, rim):
        flat = name in FLAT_FIELDS
        planes = [x + c for x, count in parts for c in range(count)]
        body = [ref[name][pl.ds(x + pad_of(name), count)].reshape(count * ny, nz) for x, count in parts]
        z_body = along_z(jnp.concatenate(body, axis=0))
        if rim:
            edges = [ref[name + "_rim"][pl.ds(x + DEEP, count)].reshape(count * SUB, nz) for x, count in parts]
            z_rim = along_z(jnp.concatenate(edges, axis=0))
        found = []
        for c, x in enumerate(planes):
            for t in range(nt + 1 if rim else nt):
                for h in range(halves):
                    v = at(name, x, t, h)
                    first, last = at(name, x, 0, h), at(name, x, nt - 1, h)
                    if t == nt:
                        before = jnp.where(sub == DEEP, pltpu.roll(last, DEEP + 1, 0), pltpu.roll(v, 1, 0))
                        after = jnp.where(sub == DEEP - 1, pltpu.roll(first, DEEP - 1, 0), pltpu.roll(v, SUB - 1, 0))
                        along = z_rim[c * SUB : (c + 1) * SUB, h * LANES : (h + 1) * LANES]
                    else:
                        if t > 0:
                            before = at(name, x, t - 1, h)
                        else:
                            if flat:
                                edge = ref[name + "_low"][x, :, span(h)]
                            else:
                                edge = pltpu.roll(at(name, x, nt, h), DEEP + 1, 0)
                            before = jnp.where(sub == 0, edge, pltpu.roll(last, 1, 0))
                        if t < nt - 1:
                            after = at(name, x, t + 1, h)
                        else:
                            if flat:
                                edge = ref[name + "_high"][x, :, span(h)]
                            else:
                                edge = pltpu.roll(at(name, x, nt, h), DEEP - 1, 0)
                            after = jnp.where(sub == SUB - 1, edge, pltpu.roll(first, SUB - 1, 0))
                        row = (c * nt + t) * SUB
                        along = z_body[row : row + SUB, h * LANES : (h + 1) * LANES]
                    sides = at(name, x - 1, t, h) + at(name, x + 1, t, h)
                    found.append((x, t, h, v, sides + (before + after) + along))
        return found

    def stage(f_in, f_out, make, parts, accs=(), rim=True, steps=1):
        f_outs = f_out if isinstance(f_out, tuple) else (f_out,) if f_out else ()

        def some(parts, accs):
            done = []
            for x, t, h, v, total in plane_sums(f_in, parts, rim):
                value, terms = make(x, t, h, v, total)
                if t == nt:
                    value = jnp.where(inside, value, 0.0)
                else:
                    accs = tuple(a + b for a, b in zip(accs, terms))
                done.append((x, t, h, value if isinstance(value, tuple) else (value,)))
            for x, t, h, values in done:
                for name, value in zip(f_outs, values):
                    put(name, x, t, h, value)
            return accs

        if steps == 1:
            return some(parts, accs)
        ((first, count),) = parts
        size = count // steps
        return lax.fori_loop(0, steps, lambda k, a: some([(first + k * size, size)], a), accs)

    def inner(f_in, f_out, make, width, accs=()):
        count = nx - 2 * (DEEP - width)
        steps = next(k for k in (4, 3, 2, 1) if count % k == 0 and count // k > 3)
        return stage(f_in, f_out, make, [(DEEP - width, count)], accs, width > 0, steps)

    def outer(f_in, f_out, make, width, accs=()):
        return stage(f_in, f_out, make, [(-width, DEEP), (nx + width - DEEP, DEEP)], accs, width > 0)

    def first_half(x, t, h, v, total):
        return at("e1", x, t, h) * v + B1 * total, ()

    def second_half(rhs):
        def make(x, t, h, v, total):
            return at("e2", x, t, h) * v + KR * at(rhs, x, t, h) + B2 * total, ()

        return make

    def strided(buf, x, t, h):
        return buf[h, x, pl.ds(t, SUB, stride=nt), :]

    def convert(i, name):
        def plane(x, carry):
            values = [(t, h, strided(raw.at[i], x, t, h)) for t in range(nt) for h in range(halves)]
            for t, h, value in values:
                put(name, x, t, h, value)
            return carry

        over(0, nx, plane)

    wait_load(1)
    convert(1, "v1a")
    wait_load(0)
    convert(0, "c1")
    pl.semaphore_wait(barrier, mx + my + 2)
    for name in ("v1a", "c1"):
        send_x(name)
        send_y(name)
    for i in (2, 3, 4):
        wait_load(i)

    def coefficients(x, t, h, damping):
        put("e1", x, t, h, K1 - B1 * damping)
        put("e2", x, t, h, K2 - B2 * damping)

    def prepare(x, acc):
        done = []
        for t in range(nt):
            for h in range(halves):
                fixed = strided(raw_act, x, t, h).astype(jnp.float32)
                opened = 1.0 - fixed
                root = lax.rsqrt(REGULAR + strided(raw.at[2], x, t, h))
                damping = opened * root
                icd = damping * root + fixed
                vb = strided(raw.at[3], x, t, h)
                va = at("v1a", x, t, h)
                acc = acc + (va * va + vb * vb * icd)
                done.append((t, h, damping, opened, icd, vb))
        for t, h, damping, opened, icd, vb in done:
            put("damp", x, t, h, damping)
            put("open", x, t, h, opened)
            put("icd", x, t, h, icd)
            put("vb", x, t, h, vb)
            coefficients(x, t, h, damping)
        return acc

    sum_ab = over(0, nx, prepare, zero)
    send_x("damp")
    send_y("damp")

    def rim_coefficients(first, last):
        def rim(x, carry):
            for h in range(halves):
                coefficients(x, nt, h, at("damp", x, nt, h))
            return carry

        over(first, last, rim)

    def outer_coefficients(first, last):
        def outside(x, carry):
            values = [(t, h, at("damp", x, t, h)) for t in range(nt) for h in range(halves)]
            for t, h, value in values:
                coefficients(x, t, h, value)
            return carry

        rim_coefficients(first, last)
        over(first, last, outside)

    ar1, ar2, ar_send, ar_recv = ref["ar1"], ref["ar2"], ref["ar_send"], ref["ar_recv"]

    def ar_copy(buf, i, phase, me, device):
        return pltpu.make_async_remote_copy(
            src_ref=buf.at[i, me],
            dst_ref=buf.at[i, me],
            send_sem=ar_send.at[i, phase],
            recv_sem=ar_recv.at[i, phase],
            device_id=device,
            device_id_type=MESH,
        )

    def ar_rows(i, rows):
        full = zero
        for k, row in enumerate(rows):
            full = jnp.where(sub == k, jnp.sum(row, axis=0, keepdims=True), full)
        ar1[i, gy] = full

        for k in far_y:
            ar_copy(ar1, i, 0, gy, (gx, lax.rem(gy + k, my))).start()

    def ar_wait(buf, i, phase, count, sem):
        whole = buf.at[i, pl.ds(0, count - 1)]
        pltpu.make_async_copy(whole, whole, sem.at[i, phase]).wait()

    def ar_middle(i):
        ar_wait(ar1, i, 0, my, ar_recv)
        full = ar1[i, 0]
        for k in range(1, my):
            full = full + ar1[i, k]
        ar2[i, gx] = full

        for k in far_x:
            ar_copy(ar2, i, 1, gx, (lax.rem(gx + k, mx), gy)).start()

    def ar_end(i, count):
        ar_wait(ar2, i, 1, mx, ar_recv)
        full = ar2[i, 0]
        for k in range(1, mx):
            full = full + ar2[i, k]
        full = jnp.sum(full, axis=1, keepdims=True)
        return [jnp.broadcast_to(full[k : k + 1], (SUB, LANES)) for k in range(count)]

    def ar_sent(i):
        ar_wait(ar1, i, 0, my, ar_send)
        ar_wait(ar2, i, 1, mx, ar_send)

    def square_out(make):
        def made(x, t, h, v, total):
            value, _ = make(x, t, h, v, total)
            return value, (value * value,)

        return made

    def state_image(x, t, h, v, total):
        return 6.0 * v - total - at("open", x, t, h) * (at("vb", x, t, h) * at("icd", x, t, h)), ()

    wait_y("v1a")
    wait_x("v1a")
    stage("v1a", "qc", state_image, [(0, DEEP), (nx - DEEP, DEEP)], rim=False)
    send_x("qc")
    stage("v1a", "qc", state_image, [(DEEP, nx - 2 * DEEP)], rim=False, steps=2)
    send_y("qc")

    def last_half(x, t, h, v, total):
        value, _ = second_half("u1")(x, t, h, v, total)
        u1 = at("u1", x, t, h)
        return value, (u1 * u1, value * at("qc", x, t, h))

    def first_chain(part, accs):
        part("c1", "half", first_half, 3)
        part("half", "u1", second_half("c1"), 2)
        part("u1", "half", first_half, 1)
        return part("half", "p1", last_half, 0, accs)

    def second_chain(part):
        part("qc", "half_q", first_half, 3)
        part("half_q", "uq", second_half("qc"), 2)
        part("uq", "half_q", first_half, 1)
        part("half_q", "p2", second_half("uq"), 0)

    merge_inner("c1")
    merge_inner("damp")
    rim_coefficients(0, nx)
    accs = first_chain(inner, (zero, zero))
    merge_inner("qc")
    second_chain(inner)

    merge_outer("c1")
    merge_outer("damp")
    outer_coefficients(1 - DEEP, 0)
    outer_coefficients(nx, nx + DEEP - 1)
    sum_u, sum_qp = first_chain(outer, accs)
    send_x("p1")
    send_y("p1")
    ar_rows(0, [sum_ab + INV2 * sum_u, sum_ab + (2.0 * INV2) * sum_qp])

    merge_outer("qc")
    ar_middle(0)
    second_chain(outer)
    send_x("p2")
    send_y("p2")

    def adjoint_image(x, t, h, v, total):
        damping = at("damp", x, t, h)
        part = 6.0 * v - total + damping * damping * at("p1", x, t, h)
        return INV2 * part + at("qc", x, t, h), ()

    def image(x, t, h, v, total):
        return 6.0 * v - total, ()

    def third_chain(part):
        part("p1", "kp", image, 3)
        part("kp", "rc", adjoint_image, 2)
        part("rc", "half", first_half, 1)
        part("half", "ur", second_half("rc"), 0)

    merge_inner("p1")
    third_chain(inner)
    wait_y("p2")
    stage("p2", "kp2", image, [(1, nx - 2)], rim=False, steps=2)
    merge_outer("p1")
    third_chain(outer)
    wait_x("p2")
    stage("p2", "kp2", image, [(0, 1), (nx - 1, 1)], rim=False)
    m0, m1 = ar_end(0, 2)
    shift = m1 / m0

    def close(x, accs):
        done = []
        for t in range(nt):
            for h in range(halves):
                va, p1 = at("v1a", x, t, h), INV2 * at("p1", x, t, h)
                icd, opened, vb = at("icd", x, t, h), at("open", x, t, h), at("vb", x, t, h)
                step, uq = INV2 * at("kp", x, t, h), at("uq", x, t, h)
                za = (va + step) - shift * va
                ra = za + INV2 * at("kp2", x, t, h) - shift * step
                v2b = (1.0 - shift) * vb - opened * p1
                zb = v2b * icd
                zc = INV2 * at("p2", x, t, h) - shift * p1
                rb = v2b - opened * zc
                rc = at("rc", x, t, h) - shift * at("qc", x, t, h)
                u2 = uq - shift * at("u1", x, t, h)
                ur = at("ur", x, t, h) - shift * uq
                base = za * za + zb * v2b
                terms = (
                    base + INV2 * (u2 * u2),
                    base + 2.0 * (rc * zc),
                    ra * ra + rb * rb * icd + INV2 * (ur * ur),
                )
                accs = tuple(a + b for a, b in zip(accs, terms))
                done.append((t, h, (va, vb * icd, p1, za, zb, zc)))
        for t, h, values in done:
            for name, value in zip(HANDED_ON, values):
                put(name, x, t, h, value)
        return accs

    sums = over(0, nx, close, (zero, zero, zero))
    ar_rows(1, sums)
    for name in DEEP_FIELDS + FLAT_FIELDS:
        wait_sent(name)
    ar_sent(0)
    ar_middle(1)
    n2, top, m4 = ar_end(1, 3)

    d2 = top / n2
    g2sq = n2 / m0
    g2 = jnp.sqrt(g2sq)
    g3sq = jnp.maximum(m4 / n2 - d2 * d2 - g2sq, 0.0)
    a1 = jnp.sqrt(shift * shift + g2sq)
    c2, s2 = shift / a1, g2 / a1
    b0 = c2 * d2 - s2 * g2
    b1 = jnp.sqrt(b0 * b0 + g3sq)
    b2 = s2 * d2 + c2 * g2
    c3 = b0 / b1
    ref["coef"][0] = (c2 + c3 * s2 * b2 / b1) / a1
    ref["coef"][1] = -c3 / (b1 * a1)
    ar_sent(1)


def combine(nx, ny, nz, pa, pb, pc, za, zb, zc, coef, out_a, out_b, out_c, raw, out_sem):
    nt, halves, parts = ny // SUB, nz // LANES, 4
    on_p, on_z = coef[0], coef[1]
    outs = ((pa, za, out_a), (pb, zb, out_b), (pc, zc, out_c))

    def finish(x, carry):
        done = []
        for i, (p, z, _) in enumerate(outs):
            for t in range(nt):
                for h in range(halves):
                    span = pl.ds(h * LANES, LANES)
                    done.append((i, t, h, on_p * p[x, t, :, span] + on_z * z[x, t, :, span]))
        for i, t, h, value in done:
            raw[i, h, x, pl.ds(t, SUB, stride=nt), :] = value
        return carry

    size = nx // parts
    stores = []
    for part in range(parts):
        lax.fori_loop(part * size, (part + 1) * size, finish, 0)
        for i, (_, _, out) in enumerate(outs):
            rows = pl.ds(part * size, size)
            for h in range(halves):
                to = out.at[rows, :, pl.ds(h * LANES, LANES)]
                store = pltpu.make_async_copy(raw.at[i, h, rows], to, out_sem.at[i, part, h])
                store.start()
                stores.append(store)
    for store in stores:
        store.wait()


def shards(va, vb, vc, barrier, active):
    nx, ny, nz = va.shape
    nt, halves = ny // SUB, nz // LANES
    f32 = jnp.float32
    hbm = pl.BlockSpec(memory_space=pltpu.HBM)
    vmem = pl.BlockSpec(memory_space=pltpu.VMEM)
    shapes = scratch(nx, ny, nz, lax.axis_size("gx"), lax.axis_size("gy"))
    handed = (jax.ShapeDtypeStruct((nx, nt, SUB, nz), f32),) * len(HANDED_ON)
    handed += (jax.ShapeDtypeStruct((2, SUB, LANES), f32),)
    found = pl.pallas_call(
        functools.partial(kernel, nx, ny, nz, tuple(shapes)),
        out_shape=handed,
        in_specs=[hbm] * 5,
        out_specs=(vmem,) * len(handed),
        scratch_shapes=list(shapes.values()),
        compiler_params=pltpu.CompilerParams(
            collective_id=0, has_side_effects=True, vmem_limit_bytes=47 * 1024 * 1024
        ),
    )(va, vb, vc, barrier, active)
    out = jax.ShapeDtypeStruct(va.shape, f32)
    return pl.pallas_call(
        functools.partial(combine, nx, ny, nz),
        out_shape=(out,) * 3,
        in_specs=[vmem] * len(handed),
        out_specs=(hbm,) * 3,
        scratch_shapes=[pltpu.VMEM((3, halves, nx, ny, LANES), f32), pltpu.SemaphoreType.DMA((3, 4, halves))],
        compiler_params=pltpu.CompilerParams(vmem_limit_bytes=6 * 1024 * 1024),
    )(*found)


def solution(mesh):
    placed = P("gx", "gy", None)
    return jax.shard_map(
        shards,
        mesh=mesh,
        in_specs=(placed,) * 5,
        out_specs=(placed,) * 3,
        check_vma=False,
    )
```

```python
import functools

import jax
import jax.numpy as jnp
from jax import lax
from jax.experimental import pallas as pl
from jax.experimental.pallas import tpu as pltpu
from jax.sharding import PartitionSpec as P

REGULAR = 0.01
CENTRE = 8.0
HALF = 7.5
STRETCH = CENTRE / HALF
Q0 = 1.0 / STRETCH
Q1 = 1.0 / (2.0 * STRETCH - Q0)
Q2 = 1.0 / (2.0 * STRETCH - Q1)
A1, B1 = Q1 * Q0, 2.0 * Q1 / HALF
A2, B2 = Q2 * Q1, 2.0 * Q2 / HALF
K1 = 1.0 + A1 + B1 * (CENTRE - 6.0)
K2 = 1.0 + A2 - 6.0 * B2
KR = B2 * CENTRE - A2
INV = 1.0 / CENTRE
INV2 = INV * INV

LANES = 128
SUB = 8
DEEP = 4
MESH = pl.DeviceIdType.MESH
WAYS = ((1, 0), (-1, 0), (0, 1), (0, -1), (1, 1), (-1, 1), (1, -1), (-1, -1))
DEEP_FIELDS = ("c1", "damp", "qc", "p1")
FLAT_FIELDS = ("v1a", "p2")
LOCAL_FIELDS = ("half", "half_q", "u1", "uq", "kp", "rc", "e1", "e2")
OWN_FIELDS = ("open", "icd", "vb", "ur", "kp2")
HANDED_ON = ("pa", "pb", "pc", "za", "zb", "zc")


def scratch(nx, ny, nz, mx, my):
    f32 = jnp.float32
    nt, halves = ny // SUB, nz // LANES
    shapes = {
        "raw": pltpu.VMEM((4, halves, nx, ny, LANES), f32),
        "raw_act": pltpu.VMEM((halves, nx, ny, LANES), jnp.int32),
        "ar1": pltpu.VMEM((2, my, SUB, LANES), f32),
        "ar2": pltpu.VMEM((2, mx, SUB, LANES), f32),
        "in_sem": pltpu.SemaphoreType.DMA((5, halves)),
        "half_send": pltpu.SemaphoreType.DMA((2,)),
        "half_recv": pltpu.SemaphoreType.DMA((2,)),
        "half_q_send": pltpu.SemaphoreType.DMA((2,)),
        "half_q_recv": pltpu.SemaphoreType.DMA((2,)),
        "ar_send": pltpu.SemaphoreType.DMA((2, 2)),
        "ar_recv": pltpu.SemaphoreType.DMA((2, 2)),
    }
    shapes["band"] = pltpu.VMEM((nz, nz), jnp.bfloat16)
    for name in DEEP_FIELDS + LOCAL_FIELDS:
        shapes[name] = pltpu.VMEM((nx + 2 * DEEP, nt, SUB, nz), f32)
        shapes[name + "_rim"] = pltpu.VMEM((nx + 2 * DEEP, SUB, nz), f32)
    for name in FLAT_FIELDS:
        shapes[name] = pltpu.VMEM((nx + 2, nt, SUB, nz), f32)
    for name in OWN_FIELDS:
        shapes[name] = pltpu.VMEM((nx, nt, SUB, nz), f32)
    for name in DEEP_FIELDS + FLAT_FIELDS:
        rows, pad = (DEEP, DEEP) if name in DEEP_FIELDS else (1, 0)
        for side in ("_low", "_high"):
            shapes[name + side] = pltpu.VMEM((nx + 2 * pad, rows, nz), f32)
        for side in ("_down", "_up"):
            shapes[name + side] = pltpu.VMEM((nx, rows, nz), f32)
        shapes[name + "_send"] = pltpu.SemaphoreType.DMA((8,))
        shapes[name + "_recv"] = pltpu.SemaphoreType.DMA((8,))
    return shapes


def kernel(nx, ny, nz, names, va_in, vb_in, vc_in, bar_in, act_in, *refs):
    ref = dict(zip(HANDED_ON + ("coef",) + names, refs))
    raw, raw_act = ref["raw"], ref["raw_act"]
    gx, gy = lax.axis_index("gx"), lax.axis_index("gy")
    mx, my = lax.axis_size("gx"), lax.axis_size("gy")
    nt = ny // SUB
    halves = nz // LANES

    inputs = ((vc_in, raw.at[0]), (va_in, raw.at[1]), (act_in, raw_act), (bar_in, raw.at[2]), (vb_in, raw.at[3]))
    loads = [
        [
            pltpu.make_async_copy(src.at[:, :, pl.ds(h * LANES, LANES)], dst.at[h], ref["in_sem"].at[i, h])
            for h in range(halves)
        ]
        for i, (src, dst) in enumerate(inputs)
    ]
    for load in loads:
        for part in load:
            part.start()

    def wait_load(i):
        for part in loads[i]:
            part.wait()

    barrier = pltpu.get_barrier_semaphore()

    def greet(sx, sy):
        device = (lax.rem(gx + sx, mx), lax.rem(gy + sy, my))
        pl.semaphore_signal(barrier, inc=1, device_id=device, device_id_type=MESH)

    far_x = sorted(range(1, mx), key=lambda k: abs(2 * k - mx))
    far_y = sorted(range(1, my), key=lambda k: abs(2 * k - my))
    for k in far_x:
        greet(k, 0)
    for sx in (1, mx - 1):
        for sy in (1, my - 1):
            greet(sx, sy)
    for k in far_y:
        greet(0, k)

    def clear(side):
        for name in DEEP_FIELDS + FLAT_FIELDS:
            edge = ref[name + side]
            edge[...] = jnp.zeros(edge.shape, jnp.float32)

    pl.when(gy == 0)(lambda: clear("_low"))
    pl.when(gy == my - 1)(lambda: clear("_high"))

    sub = lax.broadcasted_iota(jnp.int32, (SUB, LANES), 0)
    zero = jnp.zeros((SUB, LANES), jnp.float32)
    inside = jnp.where(sub < DEEP, gy, my - 1 - gy) > 0

    def span(h):
        return pl.ds(h * LANES, LANES)

    def copy_to(name, way):
        sx, sy = WAYS[way]
        deep = name in DEEP_FIELDS
        pad = DEEP if deep else 1
        if sy == 0:
            depth = {"c1": DEEP - 1, "qc": DEEP - 1, "damp": DEEP - 2}.get(name, pad)
            src, dst = (nx - depth, -depth) if sx > 0 else (0, nx)
            src, dst = ref[name].at[pl.ds(src + pad, depth)], ref[name].at[pl.ds(dst + pad, depth)]
        else:
            src, dst = ref[name + ("_up" if sy > 0 else "_down")], ref[name + ("_low" if sy > 0 else "_high")]
            if sx == 0:
                dst = dst.at[pl.ds(DEEP if deep else 0, nx)]
            else:
                count = DEEP - 2 if name == "damp" else DEEP - 1
                src = src.at[pl.ds(nx - count if sx > 0 else 0, count)]
                dst = dst.at[pl.ds(DEEP - count if sx > 0 else nx + DEEP, count)]
        return pltpu.make_async_remote_copy(
            src_ref=src,
            dst_ref=dst,
            send_sem=ref[name + "_send"].at[way],
            recv_sem=ref[name + "_recv"].at[way],
            device_id=(lax.rem(gx + mx + sx, mx), gy + sy),
            device_id_type=MESH,
        )

    def send_x(name):
        copy_to(name, 0).start()
        copy_to(name, 1).start()

    def along_y(name, act, taking, ways):
        for step in (1, -1):

            @pl.when(gy < my - 1 if (step > 0) != taking else gy > 0)
            def _():
                for way in ways:
                    if WAYS[way][1] == step:
                        act(copy_to(name, way))

    def all_ways(name):
        return range(2, 8 if name in DEEP_FIELDS else 4)

    def send_y(name):
        along_y(name, lambda copy: copy.start(), False, all_ways(name))

    def wait_y(name):
        along_y(name, lambda copy: copy.wait_recv(), True, (2, 3))

    def wait_x(name):
        copy_to(name, 0).wait_recv()
        copy_to(name, 1).wait_recv()
        if name in DEEP_FIELDS:
            along_y(name, lambda copy: copy.wait_recv(), True, (4, 5, 6, 7))

    def wait_sent(name):
        copy_to(name, 0).wait_send()
        copy_to(name, 1).wait_send()
        along_y(name, lambda copy: copy.wait_send(), False, all_ways(name))

    def half_copy(name, way):
        src, dst = (nx - DEEP + 1, 1 - DEEP) if way == 0 else (DEEP - 2, nx + DEEP - 2)
        return pltpu.make_async_remote_copy(
            src_ref=ref[name].at[src + DEEP],
            dst_ref=ref[name].at[dst + DEEP],
            send_sem=ref[name + "_send"].at[way],
            recv_sem=ref[name + "_recv"].at[way],
            device_id=(lax.rem(gx + mx + WAYS[way][0], mx), gy),
            device_id_type=MESH,
        )

    def pad_of(name):
        return DEEP if name in DEEP_FIELDS + LOCAL_FIELDS else 1 if name in FLAT_FIELDS else 0

    def at(name, x, t, h):
        if t == nt:
            return ref[name + "_rim"][x + DEEP, :, span(h)]
        return ref[name][x + pad_of(name), t, :, span(h)]

    def put(name, x, t, h, value, pack=True):
        if t == nt:
            ref[name + "_rim"][x + DEEP, :, span(h)] = value
            return
        ref[name][x + pad_of(name), t, :, span(h)] = value
        if not pack:
            return
        if name in DEEP_FIELDS:
            if t < DEEP:
                ref[name + "_down"][x, t : t + 1, span(h)] = value[0:1]
            if t >= nt - DEEP:
                ref[name + "_up"][x, t - nt + DEEP : t - nt + DEEP + 1, span(h)] = value[SUB - 1 : SUB]
        elif name in FLAT_FIELDS:
            if t == 0:
                ref[name + "_down"][x, :, span(h)] = value[0:1]
            if t == nt - 1:
                ref[name + "_up"][x, :, span(h)] = value[SUB - 1 : SUB]

    def over(first, last, plane, carry=0):
        return lax.fori_loop(0, last - first, lambda k, c: plane(k + first, c), carry)

    def merge(name, first, last):
        def plane(x, carry):
            for h in range(halves):
                low, high = ref[name + "_low"][x, :, span(h)], ref[name + "_high"][x, :, span(h)]
                ref[name + "_rim"][x, :, span(h)] = jnp.concatenate([low, high], axis=0)
            return carry

        over(first + DEEP, last + DEEP, plane)

    def merge_inner(name):
        wait_y(name)
        merge(name, 0, nx)

    def merge_outer(name):
        wait_x(name)
        merge(name, -DEEP, 0)
        merge(name, nx, nx + DEEP)

    rows = lax.broadcasted_iota(jnp.int32, (nz, nz), 0)
    columns = lax.broadcasted_iota(jnp.int32, (nz, nz), 1)
    ref["band"][...] = jnp.where(jnp.abs(rows - columns) == 1, 1.0, 0.0).astype(jnp.bfloat16)

    def along_z(values):
        top = values.astype(jnp.bfloat16)
        rest = (values - top.astype(jnp.float32)).astype(jnp.bfloat16)
        band = ref["band"][...]
        return jnp.dot(top, band, preferred_element_type=jnp.float32) + jnp.dot(
            rest, band, preferred_element_type=jnp.float32
        )

    def plane_sums(name, parts, rim):
        flat = name in FLAT_FIELDS
        planes = [x + c for x, count in parts for c in range(count)]
        body = [ref[name][pl.ds(x + pad_of(name), count)].reshape(count * ny, nz) for x, count in parts]
        z_body = along_z(jnp.concatenate(body, axis=0))
        if rim:
            edges = [ref[name + "_rim"][pl.ds(x + DEEP, count)].reshape(count * SUB, nz) for x, count in parts]
            z_rim = along_z(jnp.concatenate(edges, axis=0))
        found = []
        for c, x in enumerate(planes):
            for t in range(nt + 1 if rim else nt):
                for h in range(halves):
                    v = at(name, x, t, h)
                    first, last = at(name, x, 0, h), at(name, x, nt - 1, h)
                    if t == nt:
                        before = jnp.where(sub == DEEP, pltpu.roll(last, DEEP + 1, 0), pltpu.roll(v, 1, 0))
                        after = jnp.where(sub == DEEP - 1, pltpu.roll(first, DEEP - 1, 0), pltpu.roll(v, SUB - 1, 0))
                        along = z_rim[c * SUB : (c + 1) * SUB, h * LANES : (h + 1) * LANES]
                    else:
                        if t > 0:
                            before = at(name, x, t - 1, h)
                        else:
                            if flat:
                                edge = ref[name + "_low"][x, :, span(h)]
                            else:
                                edge = pltpu.roll(at(name, x, nt, h), DEEP + 1, 0)
                            before = jnp.where(sub == 0, edge, pltpu.roll(last, 1, 0))
                        if t < nt - 1:
                            after = at(name, x, t + 1, h)
                        else:
                            if flat:
                                edge = ref[name + "_high"][x, :, span(h)]
                            else:
                                edge = pltpu.roll(at(name, x, nt, h), DEEP - 1, 0)
                            after = jnp.where(sub == SUB - 1, edge, pltpu.roll(first, SUB - 1, 0))
                        row = (c * nt + t) * SUB
                        along = z_body[row : row + SUB, h * LANES : (h + 1) * LANES]
                    sides = at(name, x - 1, t, h) + at(name, x + 1, t, h)
                    found.append((x, t, h, v, sides + (before + after) + along))
        return found

    def stage(f_in, f_out, make, parts, accs=(), rim=True, steps=1):
        f_outs = f_out if isinstance(f_out, tuple) else (f_out,) if f_out else ()

        def some(parts, accs):
            done = []
            for x, t, h, v, total in plane_sums(f_in, parts, rim):
                value, terms = make(x, t, h, v, total)
                if t == nt:
                    value = jnp.where(inside, value, 0.0)
                else:
                    accs = tuple(a + b for a, b in zip(accs, terms))
                done.append((x, t, h, value if isinstance(value, tuple) else (value,)))
            for x, t, h, values in done:
                for name, value in zip(f_outs, values):
                    put(name, x, t, h, value)
            return accs

        if steps == 1:
            return some(parts, accs)
        ((first, count),) = parts
        size = count // steps
        return lax.fori_loop(0, steps, lambda k, a: some([(first + k * size, size)], a), accs)

    def inner(f_in, f_out, make, width, accs=()):
        count = nx - 2 * (DEEP - width)
        steps = next(k for k in (4, 3, 2, 1) if count % k == 0 and count // k > 3)
        return stage(f_in, f_out, make, [(DEEP - width, count)], accs, width > 0, steps)

    def outer(f_in, f_out, make, width, accs=()):
        return stage(f_in, f_out, make, [(-width, DEEP), (nx + width - DEEP, DEEP)], accs, width > 0)

    def first_half(x, t, h, v, total):
        return at("e1", x, t, h) * v + B1 * total, ()

    def second_half(rhs):
        def make(x, t, h, v, total):
            return at("e2", x, t, h) * v + KR * at(rhs, x, t, h) + B2 * total, ()

        return make

    def strided(buf, x, t, h):
        return buf[h, x, pl.ds(t, SUB, stride=nt), :]

    def convert(i, name):
        def plane(x, carry):
            values = [(t, h, strided(raw.at[i], x, t, h)) for t in range(nt) for h in range(halves)]
            for t, h, value in values:
                put(name, x, t, h, value)
            return carry

        over(0, nx, plane)

    wait_load(1)
    convert(1, "v1a")
    wait_load(0)
    convert(0, "c1")
    for i in (2, 3, 4):
        wait_load(i)

    def coefficients(x, t, h, damping):
        put("e1", x, t, h, K1 - B1 * damping)
        put("e2", x, t, h, K2 - B2 * damping)

    def prepare(x, acc):
        done = []
        for t in range(nt):
            for h in range(halves):
                fixed = strided(raw_act, x, t, h).astype(jnp.float32)
                opened = 1.0 - fixed
                root = lax.rsqrt(REGULAR + strided(raw.at[2], x, t, h))
                damping = opened * root
                icd = damping * root + fixed
                vb = strided(raw.at[3], x, t, h)
                va = at("v1a", x, t, h)
                acc = acc + (va * va + vb * vb * icd)
                done.append((t, h, damping, opened, icd, vb))
        for t, h, damping, opened, icd, vb in done:
            put("damp", x, t, h, damping)
            put("open", x, t, h, opened)
            put("icd", x, t, h, icd)
            put("vb", x, t, h, vb)
            coefficients(x, t, h, damping)
        return acc

    sum_ab = over(0, nx, prepare, zero)
    pl.semaphore_wait(barrier, mx + my + 2)
    for name in ("v1a", "c1", "damp"):
        send_x(name)
        send_y(name)

    def rim_coefficients(first, last):
        def rim(x, carry):
            for h in range(halves):
                coefficients(x, nt, h, at("damp", x, nt, h))
            return carry

        over(first, last, rim)

    def outer_coefficients(first, last):
        def outside(x, carry):
            values = [(t, h, at("damp", x, t, h)) for t in range(nt) for h in range(halves)]
            for t, h, value in values:
                coefficients(x, t, h, value)
            return carry

        rim_coefficients(first, last)
        over(first, last, outside)

    ar1, ar2, ar_send, ar_recv = ref["ar1"], ref["ar2"], ref["ar_send"], ref["ar_recv"]

    def ar_copy(buf, i, phase, me, device):
        return pltpu.make_async_remote_copy(
            src_ref=buf.at[i, me],
            dst_ref=buf.at[i, me],
            send_sem=ar_send.at[i, phase],
            recv_sem=ar_recv.at[i, phase],
            device_id=device,
            device_id_type=MESH,
        )

    def ar_rows(i, rows):
        full = zero
        for k, row in enumerate(rows):
            full = jnp.where(sub == k, jnp.sum(row, axis=0, keepdims=True), full)
        ar1[i, gy] = full

        for k in far_y:
            ar_copy(ar1, i, 0, gy, (gx, lax.rem(gy + k, my))).start()

    def ar_wait(buf, i, phase, count, sem):
        whole = buf.at[i, pl.ds(0, count - 1)]
        pltpu.make_async_copy(whole, whole, sem.at[i, phase]).wait()

    def ar_middle(i):
        ar_wait(ar1, i, 0, my, ar_recv)
        full = ar1[i, 0]
        for k in range(1, my):
            full = full + ar1[i, k]
        ar2[i, gx] = full

        for k in far_x:
            ar_copy(ar2, i, 1, gx, (lax.rem(gx + k, mx), gy)).start()

    def ar_end(i, count):
        ar_wait(ar2, i, 1, mx, ar_recv)
        full = ar2[i, 0]
        for k in range(1, mx):
            full = full + ar2[i, k]
        full = jnp.sum(full, axis=1, keepdims=True)
        return [jnp.broadcast_to(full[k : k + 1], (SUB, LANES)) for k in range(count)]

    def ar_sent(i):
        ar_wait(ar1, i, 0, my, ar_send)
        ar_wait(ar2, i, 1, mx, ar_send)

    def square_out(make):
        def made(x, t, h, v, total):
            value, _ = make(x, t, h, v, total)
            return value, (value * value,)

        return made

    def state_image(x, t, h, v, total):
        return 6.0 * v - total - at("open", x, t, h) * (at("vb", x, t, h) * at("icd", x, t, h)), ()

    def last_half(x, t, h, v, total):
        value, _ = second_half("u1")(x, t, h, v, total)
        u1 = at("u1", x, t, h)
        return value, (u1 * u1, value * at("qc", x, t, h))

    def first_chain(part, accs):
        part("half", "u1", second_half("c1"), 2)
        part("u1", "half", first_half, 1)
        return part("half", "p1", last_half, 0, accs)

    def second_chain(part):
        part("half_q", "uq", second_half("qc"), 2)

    def second_chain_end(part):
        part("uq", "half_q", first_half, 1)
        part("half_q", "p2", second_half("uq"), 0)

    merge_inner("c1")
    merge_inner("damp")
    rim_coefficients(0, nx)
    def start_inner(rhs, half):
        stage(rhs, half, first_half, [(DEEP - 2, 1), (nx - DEEP + 1, 1)])
        half_copy(half, 0).start()
        half_copy(half, 1).start()

    def rest_inner(rhs, half):
        stage(rhs, half, first_half, [(1, 1), (nx - 2, 1)])
        stage(rhs, half, first_half, [(DEEP - 1, nx - 2 * DEEP + 2)], steps=2)

    def start_outer(rhs, half):
        stage(rhs, half, first_half, [(2 - DEEP, DEEP - 1), (nx - 1, DEEP - 1)])
        half_copy(half, 0).wait()
        half_copy(half, 1).wait()

    start_inner("c1", "half")

    wait_y("v1a")
    wait_x("v1a")
    stage("v1a", "qc", state_image, [(0, DEEP), (nx - DEEP, DEEP)], rim=False)
    send_x("qc")
    stage("v1a", "qc", state_image, [(DEEP, nx - 2 * DEEP)], rim=False, steps=2)
    send_y("qc")

    rest_inner("c1", "half")
    accs = first_chain(inner, (zero, zero))
    merge_inner("qc")
    start_inner("qc", "half_q")
    rest_inner("qc", "half_q")
    second_chain(inner)

    merge_outer("c1")
    merge_outer("damp")
    outer_coefficients(2 - DEEP, 0)
    outer_coefficients(nx, nx + DEEP - 2)
    start_outer("c1", "half")
    sum_u, sum_qp = first_chain(outer, accs)
    send_x("p1")
    send_y("p1")
    ar_rows(0, [sum_ab + INV2 * sum_u, sum_ab + (2.0 * INV2) * sum_qp])

    second_chain_end(inner)
    merge_outer("qc")
    start_outer("qc", "half_q")
    second_chain(outer)
    second_chain_end(outer)
    send_x("p2")
    send_y("p2")
    ar_middle(0)

    def adjoint_image(x, t, h, v, total):
        damping = at("damp", x, t, h)
        part = 6.0 * v - total + damping * damping * at("p1", x, t, h)
        return INV2 * part + at("qc", x, t, h), ()

    def image(x, t, h, v, total):
        return 6.0 * v - total, ()

    def third_chain(part):
        part("p1", "kp", image, 3)
        part("kp", "rc", adjoint_image, 2)
        part("rc", "half", first_half, 1)
        part("half", "ur", second_half("rc"), 0)

    merge_inner("p1")
    third_chain(inner)
    wait_y("p2")
    stage("p2", "kp2", image, [(1, nx - 2)], rim=False, steps=2)
    merge_outer("p1")
    third_chain(outer)
    wait_x("p2")
    stage("p2", "kp2", image, [(0, 1), (nx - 1, 1)], rim=False)
    m0, m1 = ar_end(0, 2)
    shift = m1 / m0

    def close(x, accs):
        done = []
        for t in range(nt):
            for h in range(halves):
                va, p1 = at("v1a", x, t, h), INV2 * at("p1", x, t, h)
                icd, opened, vb = at("icd", x, t, h), at("open", x, t, h), at("vb", x, t, h)
                step, uq = INV2 * at("kp", x, t, h), at("uq", x, t, h)
                za = (va + step) - shift * va
                ra = za + INV2 * at("kp2", x, t, h) - shift * step
                v2b = (1.0 - shift) * vb - opened * p1
                zb = v2b * icd
                zc = INV2 * at("p2", x, t, h) - shift * p1
                rb = v2b - opened * zc
                rc = at("rc", x, t, h) - shift * at("qc", x, t, h)
                u2 = uq - shift * at("u1", x, t, h)
                ur = at("ur", x, t, h) - shift * uq
                base = za * za + zb * v2b
                terms = (
                    base + INV2 * (u2 * u2),
                    base + 2.0 * (rc * zc),
                    ra * ra + rb * rb * icd + INV2 * (ur * ur),
                )
                accs = tuple(a + b for a, b in zip(accs, terms))
                done.append((t, h, (va, vb * icd, p1, za, zb, zc)))
        for t, h, values in done:
            for name, value in zip(HANDED_ON, values):
                put(name, x, t, h, value)
        return accs

    sums = over(0, nx, close, (zero, zero, zero))
    ar_rows(1, sums)
    for name in DEEP_FIELDS + FLAT_FIELDS:
        wait_sent(name)
    ar_sent(0)
    ar_middle(1)
    n2, top, m4 = ar_end(1, 3)

    d2 = top / n2
    g2sq = n2 / m0
    g2 = jnp.sqrt(g2sq)
    g3sq = jnp.maximum(m4 / n2 - d2 * d2 - g2sq, 0.0)
    a1 = jnp.sqrt(shift * shift + g2sq)
    c2, s2 = shift / a1, g2 / a1
    b0 = c2 * d2 - s2 * g2
    b1 = jnp.sqrt(b0 * b0 + g3sq)
    b2 = s2 * d2 + c2 * g2
    c3 = b0 / b1
    ref["coef"][0] = (c2 + c3 * s2 * b2 / b1) / a1
    ref["coef"][1] = -c3 / (b1 * a1)
    ar_sent(1)


def combine(nx, ny, nz, pa, pb, pc, za, zb, zc, coef, out_a, out_b, out_c, raw, out_sem):
    nt, halves, parts = ny // SUB, nz // LANES, 4
    on_p, on_z = coef[0], coef[1]
    outs = ((pa, za, out_a), (pb, zb, out_b), (pc, zc, out_c))

    def finish(x, carry):
        done = []
        for i, (p, z, _) in enumerate(outs):
            for t in range(nt):
                for h in range(halves):
                    span = pl.ds(h * LANES, LANES)
                    done.append((i, t, h, on_p * p[x, t, :, span] + on_z * z[x, t, :, span]))
        for i, t, h, value in done:
            raw[i, h, x, pl.ds(t, SUB, stride=nt), :] = value
        return carry

    size = nx // parts
    stores = []
    for part in range(parts):
        lax.fori_loop(part * size, (part + 1) * size, finish, 0)
        for i, (_, _, out) in enumerate(outs):
            rows = pl.ds(part * size, size)
            for h in range(halves):
                to = out.at[rows, :, pl.ds(h * LANES, LANES)]
                store = pltpu.make_async_copy(raw.at[i, h, rows], to, out_sem.at[i, part, h])
                store.start()
                stores.append(store)
    for store in stores:
        store.wait()


def shards(va, vb, vc, barrier, active):
    nx, ny, nz = va.shape
    nt, halves = ny // SUB, nz // LANES
    f32 = jnp.float32
    hbm = pl.BlockSpec(memory_space=pltpu.HBM)
    vmem = pl.BlockSpec(memory_space=pltpu.VMEM)
    shapes = scratch(nx, ny, nz, lax.axis_size("gx"), lax.axis_size("gy"))
    handed = (jax.ShapeDtypeStruct((nx, nt, SUB, nz), f32),) * len(HANDED_ON)
    handed += (jax.ShapeDtypeStruct((2, SUB, LANES), f32),)
    found = pl.pallas_call(
        functools.partial(kernel, nx, ny, nz, tuple(shapes)),
        out_shape=handed,
        in_specs=[hbm] * 5,
        out_specs=(vmem,) * len(handed),
        scratch_shapes=list(shapes.values()),
        compiler_params=pltpu.CompilerParams(
            collective_id=0, has_side_effects=True, vmem_limit_bytes=47 * 1024 * 1024
        ),
    )(va, vb, vc, barrier, active)
    out = jax.ShapeDtypeStruct(va.shape, f32)
    return pl.pallas_call(
        functools.partial(combine, nx, ny, nz),
        out_shape=(out,) * 3,
        in_specs=[vmem] * len(handed),
        out_specs=(hbm,) * 3,
        scratch_shapes=[pltpu.VMEM((3, halves, nx, ny, LANES), f32), pltpu.SemaphoreType.DMA((3, 4, halves))],
        compiler_params=pltpu.CompilerParams(vmem_limit_bytes=6 * 1024 * 1024),
    )(*found)


def solution(mesh):
    placed = P("gx", "gy", None)
    return jax.shard_map(
        shards,
        mesh=mesh,
        in_specs=(placed,) * 5,
        out_specs=(placed,) * 3,
        check_vma=False,
    )
```
